128 devices in a mesh: dp: 32 (over x_hi, z, y), tensor: 4 (over x_lo, core).
Axes of the slice: x: 4 (x_hi: 2, x_lo: 2; x = x_hi * 2 + x_lo), y: 4, z: 4, core: 2. Of those that a mesh axis runs over, the one named last changes fastest.
Arguments:
- routes: int32 [16384, 8], P(('dp', 'tensor')), may hold values from 0 to 127, all different within a row; in each aligned block of 128 rows (0 to 127, 128 to 255, ...) at most 12 rows name the same one
- gate_values: bfloat16 [16384, 8], P(('dp', 'tensor')), may hold values from 0.049804688 to 0.5
- grad_out: bfloat16 [16384, 4096], P(('dp', 'tensor')), may hold values from -0.29882812 to 0.29882812
- hidden: bfloat16 [128, 1536, 768], P(('dp', 'tensor')), may hold values from -6 to 6
- w_down: bfloat16 [128, 768, 4096], P(('dp', 'tensor')), may hold values from -0.21875 to 0.21875
Outputs:
- grad_gates: float32 [16384, 8], P(('dp', 'tensor'))
- grad_hidden: bfloat16 [128, 1536, 768], P(('dp', 'tensor'))
- grad_down: bfloat16 [128, 768, 4096], P(('dp', 'tensor'))
The draws below stay inside these ranges and needn't reach their ends.
Inputs may be any that keep to these rules, and one draw needn't show every extreme that they name: `routes`: the 8 ids of a token differ. Among the tokens of one device no expert is named more than 12 times, and in every draw some expert is named exactly 12 times by the tokens of some device.
All inputs are finite; a program needn't handle non-finite values.
Results may differ from the reference program's by a relative error of at most 0.0049.
Values may be sent and summed in bfloat16 or wider, within the bound.
A program may use at most 128 MiB of HBM per device.

```python
import math
import jax
import jax.numpy as jnp
import numpy as np
from jax import lax

D = 4096
FFE = 768
TOP = 8
TOK_DEV = 128
EXPERTS = 128
TOKENS = 16384
CAP = 12


def levels(rng, shape, cuts, least, top_value):
    factor_of = 1.0
    for dim, parts in cuts:
        draws = jax.random.uniform(jax.random.fold_in(jax.random.fold_in(rng, 6), dim), (parts,), jnp.float32, least / len(cuts), top_value / len(cuts))
        factor_of = factor_of * jnp.repeat(jnp.exp(draws), shape[dim] // parts).reshape((-1,) + (1,) * (len(shape) - 1 - dim))
    return factor_of


def routed_block(stream_key, own, number, rows, number_of, top, most, slope):
    sequence = jax.random.permutation(stream_key, number_of)
    crowded, ordinary = shares(number_of, rows * top, most, slope, True), shares(number_of, rows * top, most, slope, False)
    places = jnp.arange(number_of)

    def named(lengths, rotation):
        used = int((lengths > 0).sum())
        fixed = max(1, used // 4)
        passed = fixed + (places - fixed + rotation * (used - fixed)) % max(1, number_of - fixed)
        return jnp.zeros((number_of,), jnp.int32).at[sequence[jnp.where(places < fixed, places, passed)]].set(jnp.asarray(lengths, jnp.int32))

    lengths = jnp.where(number % 4 == 0, named(crowded, number // 4), named(ordinary, number - number // 4 - 1))
    mixed = jax.random.permutation(jax.random.fold_in(own, 3), number_of)
    giver, receiver = mixed[0:number_of // 2 * 2:2], mixed[1:number_of // 2 * 2:2]
    slack = jnp.minimum(lengths[giver] - 1, most - lengths[receiver]) // 2
    slack = jnp.where((giver == sequence[0]) | (receiver == sequence[0]) | (lengths[receiver] == 0), 0, jnp.maximum(slack, 0))
    passed = jax.random.randint(jax.random.fold_in(own, 4), (number_of // 2,), 0, 1 << 20) % (slack + 1)
    lengths = lengths.at[giver].add(-passed).at[receiver].add(passed)
    labels = jnp.searchsorted(jnp.cumsum(lengths), jnp.arange(rows * top), side="right").astype(jnp.int32)
    table = labels.reshape(top, rows).T
    table = table[jax.random.permutation(jax.random.fold_in(own, 1), rows)]
    rotation = jax.random.randint(jax.random.fold_in(own, 2), (rows, 1), 0, top)
    return jnp.take_along_axis(table, (jnp.arange(top)[None, :] + rotation) % top, axis=1)


def shares(count, total, reach, lean, full):
    weights = [(1 << 20) // math.isqrt(grade ** lean) + 1 for grade in range(1, count + 1)]
    largest = reach if full else min(reach, max(-(-total // count), total * weights[0] // sum(weights)))
    least = 1 if total - largest >= count - 1 else 0
    holding, spare = [largest] + [least] * (count - 1), total - largest - least * (count - 1)
    while spare > 0:
        free = [i for i in range(1, count) if holding[i] < largest] or [i for i in range(1, count) if holding[i] < reach]
        mass, left = sum([weights[i] for i in free]), spare
        for i in free:
            extra = min(reach - holding[i], max(1, left * weights[i] // mass), spare)
            holding[i] = holding[i] + extra
            spare = spare - extra
    return np.array(holding)


def gaussian(own_key, shape, spread, bound, cuts=(), kind=jnp.bfloat16):
    values = spread * jax.random.normal(own_key, shape, jnp.float32)
    if cuts:
        values = values * levels(own_key, shape, cuts, -0.22, 0.18)
    return jnp.clip(values, -bound, bound).astype(kind)


def setup_inputs(seed: int = 0) -> dict:
    seeds = jax.random.split(jax.random.key(seed), 6)
    routes_keys = jax.random.split(jax.random.fold_in(seeds[0], 1), TOKENS // TOK_DEV)
    routes_turns = jax.random.permutation(jax.random.fold_in(seeds[0], 3), TOKENS // TOK_DEV)
    routes = jax.vmap(lambda own, number: routed_block(jax.random.fold_in(seeds[0], 2), own, number, TOK_DEV, EXPERTS, TOP, CAP, 2))(routes_keys, routes_turns).reshape((TOKENS, TOP))
    gate_values = jnp.clip(jnp.exp(math.log(0.5) - 2.306499 * jax.random.uniform(seeds[1], (TOKENS, TOP), jnp.float32) ** levels(seeds[1], (TOKENS, TOP), ((0, 128),), -0.2, 0.2)), 0.049804688, 0.5).astype(jnp.bfloat16)
    grad_out = gaussian(seeds[2], (TOKENS, D), 0.05, 0.29882812, ((0, 128),))
    hidden = gaussian(seeds[3], (EXPERTS, EXPERTS * CAP, FFE), 1.0, 6.0, ((0, 128),))
    w_down = gaussian(seeds[4], (EXPERTS, FFE, D), FFE ** -0.5, 0.21875, ((0, 128),))
    return dict(routes=routes, gate_values=gate_values, grad_out=grad_out, hidden=hidden, w_down=w_down)


def slot_numbers(routes):
    blocks = routes.reshape(EXPERTS, TOK_DEV * TOP)
    onehot = (blocks[:, :, None] == jnp.arange(EXPERTS, dtype=jnp.int32)[None, None, :]).astype(jnp.int32)
    earlier = jnp.cumsum(onehot, axis=1) - onehot
    return jnp.sum(earlier * onehot, axis=2).reshape(TOKENS, TOP)


def reference(routes, gate_values, grad_out, hidden, w_down):
    slot_index = slot_numbers(routes)
    source = (jnp.arange(TOKENS, dtype=jnp.int32) // TOK_DEV)[:, None]
    target = (routes * (EXPERTS * CAP) + source * CAP + slot_index).reshape(-1).astype(jnp.int32)
    pair_count = TOKENS * TOP
    pair_ids = jnp.arange(pair_count, dtype=jnp.int32)
    token_table = jnp.full((EXPERTS * EXPERTS * CAP,), TOKENS, jnp.int32).at[target].set(pair_ids // TOP)
    pair_table = jnp.full((EXPERTS * EXPERTS * CAP,), pair_count, jnp.int32).at[target].set(pair_ids)
    token_table = token_table.reshape(EXPERTS, EXPERTS * CAP)
    pair_table = pair_table.reshape(EXPERTS, EXPERTS * CAP)
    padded_rows = jnp.concatenate([grad_out, jnp.zeros((1, D), grad_out.dtype)], axis=0)
    padded_gates = jnp.concatenate([gate_values.reshape(-1).astype(jnp.float32), jnp.zeros((1,), jnp.float32)])

    def one_expert(expert):
        recv_rows = padded_rows[token_table[expert]]
        row_scale = padded_gates[pair_table[expert]][:, None]
        back_proj = jnp.dot(recv_rows, w_down[expert].T, preferred_element_type=jnp.float32)
        stored = hidden[expert]
        slot_grad = jnp.sum(stored.astype(jnp.float32) * back_proj, axis=1)
        hidden_grad = (row_scale * back_proj).astype(jnp.bfloat16)
        scaled_rows = (row_scale * recv_rows.astype(jnp.float32)).astype(jnp.bfloat16)
        weight_grad = jnp.dot(stored.T, scaled_rows, preferred_element_type=jnp.float32).astype(jnp.bfloat16)
        return slot_grad, hidden_grad, weight_grad

    slot_grads, grad_hidden, grad_down = lax.map(one_expert, jnp.arange(EXPERTS, dtype=jnp.int32))
    grad_gates = slot_grads.reshape(-1)[target].reshape(TOKENS, TOP)
    return grad_gates, grad_hidden, grad_down
```

```python
import itertools

import jax
import jax.numpy as jnp
import numpy as np
from jax import lax
from jax.experimental import pallas as pl
from jax.experimental.pallas import tpu as pltpu
from jax.sharding import PartitionSpec as P

MESH = pl.DeviceIdType.MESH
F32 = jnp.float32
BF16 = jnp.bfloat16

DEV = 128
TOK = 128
CAP = 12
TOP = 8
LANE = 128
SEATS = 8
BLOCKS = 16
ROWS = SEATS * CAP


def half(v):
    return lax.div(v, 2)


def odd(v):
    return lax.rem(v, 2)


def near(k, v):
    return (1 - k) * (v + 1 - 2 * odd(v)) + k * (3 - v)


def far(k, v):
    return (1 - k) * (3 - v) + k * (v + 1 - 2 * odd(v))


def seat(k, v):
    return (1 - k) * odd(v) + k * half(v)


def pair(k, v):
    return (1 - k) * half(v) + k * odd(v + half(v))


def place(chip, core):
    x, y, z = chip
    return half(x) * 16 + z * 4 + y, odd(x) * 2 + core


def number(chip, core):
    dp, tensor = place(chip, core)
    return dp * 4 + tensor


def reach(k, chip, n):
    return tuple(far(k, v) if (n >> d) & 1 else v for d, v in enumerate(chip))


def block_of(k, chip, n):
    total = k * 8
    for d, v in enumerate(chip):
        own = pair(k, v)
        total = total + (1 << d) * ((1 - own) if (n >> d) & 1 else own)
    return total


def row_orders():
    natural = np.zeros(DEV * CAP, np.int32)
    for k, b, m in itertools.product(range(2), range(8), range(8)):
        chip = []
        for d in range(3):
            p, s = (b >> d) & 1, (m >> d) & 1
            chip.append((2 * p + s) if k == 0 else (2 * s + (p ^ s)))
        x, y, z = chip
        device = ((x // 2) * 16 + z * 4 + y) * 4 + (x % 2) * 2 + k
        first = ((k * 8 + b) * 8 + m) * CAP
        natural[first : first + CAP] = device * CAP + np.arange(CAP)
    kernel_row = np.argsort(natural).astype(np.int32)
    return natural, kernel_row


def iota(shape, dim):
    return lax.broadcasted_iota(jnp.int32, shape, dim)


def dot(a, b, dims=((1,), (0,))):
    return lax.dot_general(a, b, (dims, ((), ())), preferred_element_type=F32)


def ones_where(mask):
    return jnp.where(mask, 1.0, 0.0).astype(BF16)


def expand(first, gates_all, counts_all):
    row = iota((ROWS, LANE), 0)
    of = (row * 171) >> 11
    slot = (row - of * CAP).astype(F32)
    pick = ones_where(iota((ROWS, LANE), 1) == of + first)
    gates = dot(pick, gates_all)
    counts = dot(pick, counts_all)
    hit = (counts == slot) & (gates > 0.0)
    return hit, gates, of


def kernel(
    chunks,
    routes_ref,
    routes_t_ref,
    gates_t_ref,
    natural_ref,
    kernel_row_ref,
    grad_ref,
    hidden_ref,
    weight_ref,
    grad_gates_ref,
    grad_hidden_ref,
    grad_down_ref,
    tok,
    stage,
    recv,
    weight,
    hid,
    hid_k,
    hid_t,
    back,
    gcol,
    select,
    gate_f,
    gate_out,
    gate_in,
    scaled,
    down,
    sg_out,
    sg_in,
    sg_pack,
    sg_all,
    in_sem,
    rep_send,
    rep_recv,
    row_send,
    row_recv,
    gate_send,
    gate_recv,
    sg_send,
    sg_recv,
    ret_send,
    ret_recv,
    down_sem,
    hid_sem,
):
    width = recv.shape[3]
    model = weight.shape[1]
    ffe = weight.shape[0]
    dp = lax.axis_index("dp")
    tensor = lax.axis_index("tensor")
    k = odd(tensor)
    chip = (half(tensor) + 2 * lax.div(dp, 16), lax.rem(dp, 4), lax.rem(lax.div(dp, 4), 4))
    seats = tuple(seat(k, v) for v in chip)
    mine = seats[0] + 2 * seats[1] + 4 * seats[2]
    my_block = block_of(k, chip, 0)
    cores = (k, 1 - k)
    order = [(n, rc) for n in (1, 2, 4, 3, 5, 6, 7, 0) for rc in (0, 1) if (n, rc) != (0, 0)]

    def receiver(n, rc):
        return reach(k, chip, n), cores[rc]

    def sender(n, rc):
        return reach(cores[rc], chip, n), cores[rc]

    def member(flips):
        return tuple(near(k, v) if (flips >> d) & 1 else v for d, v in enumerate(chip))

    load_rows = pltpu.make_async_copy(grad_ref, tok.at[mine, :, pl.ds(0, model)], in_sem.at[0])
    load_rows.start()
    load_hidden = pltpu.make_async_copy(hidden_ref, hid, in_sem.at[1])
    load_hidden.start()
    load_weight = pltpu.make_async_copy(weight_ref, weight, in_sem.at[2])
    load_weight.start()

    barrier = pltpu.get_barrier_semaphore()
    greet = [(member(f), k) for f in range(1, 8)]
    greet += [receiver(n, rc) for n, rc in order]
    greet += [sender(n, 1) for n in range(1, 8)]
    for who, core in greet:
        pl.semaphore_signal(barrier, inc=1, device_id=place(who, core), device_id_type=MESH)

    table = jnp.zeros((DEV, TOK), F32)
    for c in range(TOP):
        named = iota((DEV, TOK), 0) == routes_t_ref[c : c + 1, :]
        table = table + jnp.where(named, gates_t_ref[c : c + 1, :], 0.0)
    tok[mine, :, pl.ds(model, LANE)] = table.astype(BF16)
    load_rows.wait()
    pl.semaphore_wait(barrier, len(greet))

    part = (model + LANE) // 3
    steps = {}
    for p in range(3):
        for s in range(3):
            axis = (p + s) % 3
            done = [(p + i) % 3 for i in range(s)]
            copies = []
            for c in range(1 << s):
                slot = 0
                for d in range(3):
                    flip = d in done and (c >> done.index(d)) & 1
                    slot = slot + (1 << d) * ((1 - seats[d]) if flip else seats[d])
                ref = tok.at[slot, :, pl.ds(p * part, part)]
                at = p * 7 + (1 << s) - 1 + c
                copies.append(
                    pltpu.make_async_remote_copy(
                        src_ref=ref,
                        dst_ref=ref,
                        send_sem=rep_send.at[at],
                        recv_sem=rep_recv.at[at],
                        device_id=place(member(1 << axis), k),
                        device_id_type=MESH,
                    )
                )
            steps[p, s] = copies
    for s in range(3):
        for p in range(3):
            if s:
                for copy in steps[p, s - 1]:
                    copy.wait_recv()
            for copy in steps[p, s]:
                copy.start()

    load_hidden.wait()
    span = 2 * LANE

    @pl.loop(0, DEV * CAP // span)
    def _(i):
        first = pl.multiple_of(i * span, span)
        move = ones_where(kernel_row_ref[0:1, :] == iota((span, DEV * CAP), 0) + first)
        moved = dot(move, hid[...])
        hid_k[pl.ds(first, span), :] = moved.astype(BF16)
        hid_t[:, pl.ds(first, span)] = moved.T.astype(BF16)

    for p in range(3):
        for copy in steps[p, 2]:
            copy.wait_recv()

    gate_f[...] = tok[:, :, pl.ds(model, LANE)].astype(F32)
    for n in range(8):
        for rc in range(2):
            expert = number(*receiver(n, rc))
            for m in range(SEATS):
                gate_out[n * 2 + rc, m : m + 1, :] = gate_f[m, pl.ds(expert, 1), :]
    gate_in[my_block] = gate_out[0]

    def gate_copy(n, rc):
        d = n * 2 + rc
        return pltpu.make_async_remote_copy(
            src_ref=gate_out.at[d],
            dst_ref=gate_in.at[my_block],
            send_sem=gate_send.at[d],
            recv_sem=gate_recv.at[my_block],
            device_id=place(*receiver(n, rc)),
            device_id_type=MESH,
        )

    for n, rc in order:
        gate_copy(n, rc).start()

    earlier = ones_where(iota((TOK, TOK), 0) < iota((TOK, TOK), 1))
    gates_all = gate_out[...].reshape(BLOCKS * SEATS, TOK)
    counts_all = dot(ones_where(gates_all > 0.0), earlier).astype(BF16)
    gates_all = gates_all.astype(BF16)
    quad = ROWS // 2

    for d in range(BLOCKS):
        hit, _, of = expand(d * SEATS, gates_all, counts_all)
        for h in range(2):
            rows = slice(h * quad, (h + 1) * quad)
            for m in range(4):
                chosen = hit[rows] & (of[rows] == 4 * h + m)
                select[h, d, :, m * TOK : (m + 1) * TOK] = ones_where(chosen)

    def row_copy(q, n, rc):
        d = n * 2 + rc
        return pltpu.make_async_remote_copy(
            src_ref=stage.at[q, d],
            dst_ref=recv.at[q, my_block],
            send_sem=row_send.at[q, d],
            recv_sem=row_recv.at[q, my_block],
            device_id=place(*receiver(n, rc)),
            device_id_type=MESH,
        )

    @pl.loop(0, chunks)
    def _(q):
        first = pl.multiple_of(q * width, width)
        for h in range(2):
            source = tok[4 * h : 4 * h + 4, :, pl.ds(first, width)].reshape(4 * TOK, width)
            picked = dot(select[h].reshape(BLOCKS * quad, 4 * TOK), source).astype(BF16)
            picked = picked.reshape(BLOCKS, quad, width)
            stage[q, :, h * quad : (h + 1) * quad, :] = picked
            recv[q, my_block, h * quad : (h + 1) * quad, :] = picked[0]
        for n, rc in order:
            row_copy(q, n, rc).start()

    for n, rc in order:
        b = block_of(cores[rc], chip, n)
        pltpu.make_async_copy(gate_in.at[b], gate_in.at[b], gate_recv.at[b]).wait()
    gates_all = gate_in[...].reshape(BLOCKS * SEATS, TOK)
    counts_all = dot(ones_where(gates_all > 0.0), earlier).astype(BF16)
    gates_all = gates_all.astype(BF16)
    for b in range(BLOCKS):
        hit, gates, _ = expand(b * SEATS, gates_all, counts_all)
        column = jnp.sum(jnp.where(hit, gates, 0.0), axis=1, keepdims=True)
        gcol[b] = jnp.broadcast_to(column, (ROWS, LANE))

    back[...] = jnp.zeros_like(back)
    load_weight.wait()

    def down_copy(q, slot):
        first = pl.multiple_of(q * width, width)
        return pltpu.make_async_copy(
            down.at[slot], grad_down_ref.at[:, pl.ds(first, width)], down_sem.at[slot]
        )

    some = BLOCKS // 2

    @pl.loop(0, chunks)
    def _(q):
        first = pl.multiple_of(q * width, width)
        slot = odd(q)
        for n, rc in order:
            b = block_of(cores[rc], chip, n)
            pltpu.make_async_copy(recv.at[q, b], recv.at[q, b], row_recv.at[q, b]).wait()

        @pl.loop(0, 2)
        def _(i):
            got = recv[q, pl.ds(i * some, some)].reshape(some * ROWS, width)
            back[pl.ds(i * some, some)] += dot(
                got, weight[:, pl.ds(first, width)], ((1,), (1,))
            ).reshape(some, ROWS, ffe)

        @pl.loop(0, BLOCKS)
        def _(b):
            wide = jnp.concatenate([gcol[b]] * (width // LANE), axis=1)
            scaled[pl.ds(b * ROWS, ROWS), :] = (recv[q, b].astype(F32) * wide).astype(BF16)

        @pl.when(q >= 2)
        def _():
            down_copy(q - 2, slot).wait()

        @pl.loop(0, width // span)
        def _(i):
            at = pl.multiple_of(i * span, span)
            down[slot, :, pl.ds(at, span)] = dot(hid_t[...], scaled[:, pl.ds(at, span)]).astype(
                BF16
            )

        down_copy(q, slot).start()

    @pl.loop(0, BLOCKS)
    def _(b):
        rows = pl.ds(b * ROWS, ROWS)
        total = back[b]
        slots = jnp.sum(hid_k[rows, :].astype(F32) * total, axis=1, keepdims=True)
        wide = jnp.concatenate([gcol[b]] * (ffe // LANE), axis=1)
        hid_k[rows, :] = (total * wide).astype(BF16)
        row = iota((ROWS, LANE), 0)
        lane = row + 4 * ((row * 171) >> 11)
        line = jnp.sum(jnp.where(iota((ROWS, LANE), 1) == lane, slots, 0.0), axis=0, keepdims=True)
        sg_out[b] = jnp.broadcast_to(line, (8, LANE))

    def slot_copy(n, rc):
        d = n * 2 + rc
        b = block_of(cores[rc], chip, n)
        return pltpu.make_async_remote_copy(
            src_ref=sg_out.at[b],
            dst_ref=sg_in.at[d],
            send_sem=sg_send.at[d],
            recv_sem=sg_recv.at[d],
            device_id=place(*sender(n, rc)),
            device_id_type=MESH,
        )

    for n, rc in order:
        slot_copy(n, rc).start()
    sg_in[0] = sg_out[my_block]

    @pl.loop(0, DEV * CAP // span)
    def _(i):
        first = pl.multiple_of(i * span, span)
        move = ones_where(natural_ref[0:1, :] == iota((span, DEV * CAP), 0) + first)
        hid[pl.ds(first, span), :] = dot(move, hid_k[...]).astype(BF16)

    store_hidden = pltpu.make_async_copy(hid, grad_hidden_ref, hid_sem.at[0])
    store_hidden.start()

    for n, rc in order:
        slot_copy(n, rc).wait_recv()
    for d in range(BLOCKS):
        sg_pack[d : d + 1, :] = sg_in[d, 0:1, :]

    def return_copy(f):
        return pltpu.make_async_remote_copy(
            src_ref=sg_pack,
            dst_ref=sg_all.at[mine],
            send_sem=ret_send.at[f],
            recv_sem=ret_recv.at[f],
            device_id=place(member(f), k),
            device_id_type=MESH,
        )

    for f in range(1, 8):
        return_copy(f).start()
    sg_all[mine] = sg_pack[...]

    column = iota((1, LANE), 1)
    chips = []
    for d in range(3):
        s = (column >> (4 + d)) & 1
        p = pair(k, chip[d])
        v = (1 - k) * (2 * p + s) + k * (2 * s + ((s + p) & 1))
        n = (column >> (1 + d)) & 1
        across = (1 - k) * (3 - v) + k * (v + 1 - 2 * (v & 1))
        chips.append(n * across + (1 - n) * v)
    x, y, z = chips
    other = column & 1
    core = other * (1 - k) + (1 - other) * k
    expert = ((x >> 1) * 16 + z * 4 + y) * 4 + (x & 1) * 2 + core
    named = [expert == routes_ref[:, c : c + 1] for c in range(TOP)]
    any_named = named[0]
    for mask in named[1:]:
        any_named = any_named | mask
    before = ones_where(iota((TOK, TOK), 1) < iota((TOK, TOK), 0))
    count = dot(before, ones_where(any_named))

    for f in range(1, 8):
        return_copy(f).wait_recv()
    turned = sg_all[...].reshape(SEATS * BLOCKS, LANE).T
    gate_f[0] = turned
    slots = gate_f[0, pl.ds(pl.multiple_of(mine * 16, 16), 16), :]
    value = jnp.zeros((TOK, LANE), F32)
    for j in range(CAP):
        value = value + jnp.where(count == float(j), slots[j : j + 1, :], 0.0)
    grad_gates_ref[...] = jnp.concatenate(
        [jnp.sum(jnp.where(mask, value, 0.0), axis=1, keepdims=True) for mask in named], axis=1
    )

    for copies in steps.values():
        for copy in copies:
            copy.wait_send()
    for n, rc in order:
        gate_copy(n, rc).wait_send()
        slot_copy(n, rc).wait_send()

    @pl.loop(0, chunks)
    def _(q):
        for n, rc in order:
            row_copy(q, n, rc).wait_send()

    for f in range(1, 8):
        return_copy(f).wait_send()
    for q in (chunks - 2, chunks - 1):
        down_copy(q, q % 2).wait()
    store_hidden.wait()


def local(routes, gate_values, grad_out, hidden, w_down):
    model = grad_out.shape[1]
    ffe = hidden.shape[2]
    slots = DEV * CAP
    width = 512
    chunks = model // width
    natural, kernel_row = (jnp.asarray(np.tile(v[None], (8, 1))) for v in row_orders())
    vmem = pl.BlockSpec(memory_space=pltpu.VMEM)
    hbm = pl.BlockSpec(memory_space=pl.ANY)
    dma = pltpu.SemaphoreType.DMA

    def body(*refs):
        kernel(chunks, *refs)

    grad_gates, grad_hidden, grad_down = pl.pallas_call(
        body,
        out_shape=(
            jax.ShapeDtypeStruct((TOK, TOP), F32),
            jax.ShapeDtypeStruct((slots, ffe), BF16),
            jax.ShapeDtypeStruct((ffe, model), BF16),
        ),
        in_specs=[vmem] * 5 + [hbm] * 3,
        out_specs=(vmem, hbm, hbm),
        scratch_shapes=[
            pltpu.VMEM((SEATS, TOK, model + LANE), BF16),
            pltpu.VMEM((chunks, BLOCKS, ROWS, width), BF16),
            pltpu.VMEM((chunks, BLOCKS, ROWS, width), BF16),
            pltpu.VMEM((ffe, model), BF16),
            pltpu.VMEM((slots, ffe), BF16),
            pltpu.VMEM((slots, ffe), BF16),
            pltpu.VMEM((ffe, slots), BF16),
            pltpu.VMEM((BLOCKS, ROWS, ffe), F32),
            pltpu.VMEM((BLOCKS, ROWS, LANE), F32),
            pltpu.VMEM((2, BLOCKS, ROWS // 2, 4 * TOK), BF16),
            pltpu.VMEM((SEATS, DEV, TOK), F32),
            pltpu.VMEM((BLOCKS, SEATS, TOK), F32),
            pltpu.VMEM((BLOCKS, SEATS, TOK), F32),
            pltpu.VMEM((slots, width), BF16),
            pltpu.VMEM((2, ffe, width), BF16),
            pltpu.VMEM((BLOCKS, 8, LANE), F32),
            pltpu.VMEM((BLOCKS, 8, LANE), F32),
            pltpu.VMEM((BLOCKS, LANE), F32),
            pltpu.VMEM((SEATS, BLOCKS, LANE), F32),
            dma((3,)),
            dma((21,)),
            dma((21,)),
            dma((chunks, BLOCKS)),
            dma((chunks, BLOCKS)),
            dma((BLOCKS,)),
            dma((BLOCKS,)),
            dma((BLOCKS,)),
            dma((BLOCKS,)),
            dma((8,)),
            dma((8,)),
            dma((2,)),
            dma((1,)),
        ],
        compiler_params=pltpu.CompilerParams(
            collective_id=0, has_side_effects=True, vmem_limit_bytes=63 * 1024 * 1024
        ),
        cost_estimate=pl.CostEstimate(
            flops=4 * slots * ffe * model, bytes_accessed=20_000_000, transcendentals=0
        ),
    )(
        routes,
        routes.T,
        gate_values.T.astype(F32),
        natural,
        kernel_row,
        grad_out,
        hidden[0],
        w_down[0],
    )
    return grad_gates, grad_hidden[None], grad_down[None]


def solution(mesh):
    both = ("dp", "tensor")
    in_specs = (P(both, None), P(both, None), P(both, None), P(both, None, None), P(both, None, None))
    out_specs = (P(both, None), P(both, None, None), P(both, None, None))
    return jax.shard_map(local, mesh=mesh, in_specs=in_specs, out_specs=out_specs, check_vma=False)
```

```python
import itertools

import jax
import jax.numpy as jnp
import numpy as np
from jax import lax
from jax.experimental import pallas as pl
from jax.experimental.pallas import tpu as pltpu
from jax.sharding import PartitionSpec as P

MESH = pl.DeviceIdType.MESH
F32 = jnp.float32
BF16 = jnp.bfloat16

DEV = 128
TOK = 128
CAP = 12
TOP = 8
LANE = 128
SEATS = 8
BLOCKS = 16
ROWS = SEATS * CAP


def half(v):
    return lax.div(v, 2)


def odd(v):
    return lax.rem(v, 2)


def near(k, v):
    return (1 - k) * (v + 1 - 2 * odd(v)) + k * (3 - v)


def far(k, v):
    return (1 - k) * (3 - v) + k * (v + 1 - 2 * odd(v))


def seat(k, v):
    return (1 - k) * odd(v) + k * half(v)


def pair(k, v):
    return (1 - k) * half(v) + k * odd(v + half(v))


def place(chip, core):
    x, y, z = chip
    return half(x) * 16 + z * 4 + y, odd(x) * 2 + core


def number(chip, core):
    dp, tensor = place(chip, core)
    return dp * 4 + tensor


def reach(k, chip, n):
    return tuple(far(k, v) if (n >> d) & 1 else v for d, v in enumerate(chip))


def block_of(k, chip, n):
    total = k * 8
    for d, v in enumerate(chip):
        own = pair(k, v)
        total = total + (1 << d) * ((1 - own) if (n >> d) & 1 else own)
    return total


def row_orders():
    natural = np.zeros(DEV * CAP, np.int32)
    for k, b, m in itertools.product(range(2), range(8), range(8)):
        chip = []
        for d in range(3):
            p, s = (b >> d) & 1, (m >> d) & 1
            chip.append((2 * p + s) if k == 0 else (2 * s + (p ^ s)))
        x, y, z = chip
        device = ((x // 2) * 16 + z * 4 + y) * 4 + (x % 2) * 2 + k
        first = ((k * 8 + b) * 8 + m) * CAP
        natural[first : first + CAP] = device * CAP + np.arange(CAP)
    return natural


def iota(shape, dim):
    return lax.broadcasted_iota(jnp.int32, shape, dim)


def dot(a, b, dims=((1,), (0,))):
    return lax.dot_general(a, b, (dims, ((), ())), preferred_element_type=F32)


def ones_where(mask):
    return jnp.where(mask, 1.0, 0.0).astype(BF16)


def expand(first, gates_all, counts_all):
    row = iota((ROWS, LANE), 0)
    of = (row * 171) >> 11
    slot = (row - of * CAP).astype(F32)
    pick = ones_where(iota((ROWS, LANE), 1) == of + first)
    gates = dot(pick, gates_all)
    counts = dot(pick, counts_all)
    hit = (counts == slot) & (gates > 0.0)
    return hit, gates, of


def kernel(
    chunks,
    routes_ref,
    gates_ref,
    kernel_row_ref,
    grad_ref,
    hidden_ref,
    weight_ref,
    grad_gates_ref,
    grad_hidden_ref,
    grad_down_ref,
    tok,
    stage,
    recv,
    weight,
    hid,
    hid_k,
    hid_t,
    back,
    natural,
    gcol,
    select,
    tables,
    gate_f,
    gate_out,
    gate_in,
    scaled,
    down,
    sg_out,
    sg_in,
    sg_pack,
    sg_all,
    owner,
    count,
    in_sem,
    tab_send,
    tab_recv,
    rep_send,
    rep_recv,
    row_send,
    row_recv,
    gate_send,
    gate_recv,
    sg_send,
    sg_recv,
    ret_send,
    ret_recv,
    down_sem,
    hid_sem,
):
    width = recv.shape[3]
    model = weight.shape[1]
    ffe = weight.shape[0]
    dp = lax.axis_index("dp")
    tensor = lax.axis_index("tensor")
    k = odd(tensor)
    chip = (half(tensor) + 2 * lax.div(dp, 16), lax.rem(dp, 4), lax.rem(lax.div(dp, 4), 4))
    seats = tuple(seat(k, v) for v in chip)
    mine = seats[0] + 2 * seats[1] + 4 * seats[2]
    my_block = block_of(k, chip, 0)
    cores = (k, 1 - k)
    order = [(n, rc) for n in (1, 2, 4, 3, 5, 6, 7, 0) for rc in (0, 1) if (n, rc) != (0, 0)]

    def receiver(n, rc):
        return reach(k, chip, n), cores[rc]

    def sender(n, rc):
        return reach(cores[rc], chip, n), cores[rc]

    def member(flips):
        return tuple(near(k, v) if (flips >> d) & 1 else v for d, v in enumerate(chip))

    to_id = {key: place(*receiver(*key)) for key in order}
    from_id = {key: place(*sender(*key)) for key in order}
    from_block = {(n, rc): block_of(cores[rc], chip, n) for n, rc in order}
    member_id = {f: place(member(f), k) for f in range(1, 8)}

    load_rows = pltpu.make_async_copy(grad_ref, tok.at[mine], in_sem.at[0])
    load_rows.start()
    load_hidden = pltpu.make_async_copy(hidden_ref, hid, in_sem.at[1])
    load_hidden.start()
    load_weight = pltpu.make_async_copy(weight_ref, weight, in_sem.at[2])
    load_weight.start()

    barrier = pltpu.get_barrier_semaphore()
    greet = list(member_id.values()) + list(to_id.values())
    greet += [from_id[n, 1] for n in range(1, 8)]
    for who in greet:
        pl.semaphore_signal(barrier, inc=1, device_id=who, device_id_type=MESH)

    gates_t = gates_ref[...].astype(F32)
    table = jnp.zeros((DEV, TOK), F32)
    for c in range(TOP):
        named = iota((DEV, TOK), 0) == routes_ref[c : c + 1, :]
        table = table + jnp.where(named, gates_t[c : c + 1, :], 0.0)
    tables[mine] = table.astype(BF16)
    load_rows.wait()
    pl.semaphore_wait(barrier, len(greet))

    def table_copy(f):
        return pltpu.make_async_remote_copy(
            src_ref=tables.at[mine],
            dst_ref=tables.at[mine],
            send_sem=tab_send.at[f],
            recv_sem=tab_recv.at[f],
            device_id=member_id[f],
            device_id_type=MESH,
        )

    tiles = model // LANE
    parts = [(0, 11), (11, 11), (22, tiles - 22)]

    def rep_copy(p, h, c):
        slot = 0
        for d in range(3):
            hop = (d - p) % 3
            slot = slot + (1 << d) * ((1 - seats[d]) if hop < h and (c >> hop) & 1 else seats[d])
        at = p * 7 + (1 << h) - 1 + c
        ref = tok.at[slot, :, pl.ds(parts[p][0] * LANE, parts[p][1] * LANE)]
        return pltpu.make_async_remote_copy(
            src_ref=ref,
            dst_ref=ref,
            send_sem=rep_send.at[at],
            recv_sem=rep_recv.at[at],
            device_id=member_id[1 << ((p + h) % 3)],
            device_id_type=MESH,
        )

    def own(p):
        for h in range(3):
            rep_copy(p, h, 0).start()

    def forward_first(p):
        rep_copy(p, 0, 0).wait_recv()
        rep_copy(p, 1, 1).start()
        rep_copy(p, 2, 1).start()
        rep_copy(p, 1, 0).wait_recv()
        rep_copy(p, 2, 2).start()

    def forward_last(p):
        rep_copy(p, 1, 1).wait_recv()
        rep_copy(p, 2, 3).start()

    def complete(p):
        for c in range(4):
            rep_copy(p, 2, c).wait_recv()

    for f in range(1, 8):
        table_copy(f).start()
    for p in range(3):
        own(p)

    for f in range(1, 8):
        table_copy(f).wait_recv()
    gate_f[...] = tables[...].astype(F32)
    for n in range(8):
        for rc in range(2):
            expert = number(*receiver(n, rc))
            for m in range(SEATS):
                gate_out[n * 2 + rc, m : m + 1, :] = gate_f[m, pl.ds(expert, 1), :]
    gate_in[my_block] = gate_out[0]

    def gate_copy(n, rc):
        d = n * 2 + rc
        return pltpu.make_async_remote_copy(
            src_ref=gate_out.at[d],
            dst_ref=gate_in.at[my_block],
            send_sem=gate_send.at[d],
            recv_sem=gate_recv.at[my_block],
            device_id=to_id[n, rc],
            device_id_type=MESH,
        )

    for n, rc in order:
        gate_copy(n, rc).start()

    for p in range(3):
        forward_first(p)

    earlier = ones_where(iota((TOK, TOK), 0) < iota((TOK, TOK), 1))
    gates_all = gate_out[...].reshape(BLOCKS * SEATS, TOK)
    counts_all = dot(ones_where(gates_all > 0.0), earlier).astype(BF16)
    gates_all = gates_all.astype(BF16)
    quad = ROWS // 2

    @pl.loop(0, BLOCKS)
    def _(d):
        hit, _, of = expand(d * SEATS, gates_all, counts_all)
        for h in range(2):
            rows = slice(h * quad, (h + 1) * quad)
            for m in range(4):
                chosen = hit[rows] & (of[rows] == 4 * h + m)
                select[h, d, :, m * TOK : (m + 1) * TOK] = ones_where(chosen)

    load_hidden.wait()
    span = 2 * LANE

    def permute_hidden(start, stop):
        @pl.loop(start, stop)
        def _(i):
            first = pl.multiple_of(i * span, span)
            move = ones_where(kernel_row_ref[0:1, :] == iota((span, DEV * CAP), 0) + first)
            moved = dot(move, hid[...])
            hid_k[pl.ds(first, span), :] = moved.astype(BF16)
            hid_t[:, pl.ds(first, span)] = moved.T.astype(BF16)

    permute_hidden(0, 2)
    for p in range(3):
        forward_last(p)
    permute_hidden(2, 6)

    def row_copy(q, n, rc):
        d = n * 2 + rc
        return pltpu.make_async_remote_copy(
            src_ref=stage.at[q, d],
            dst_ref=recv.at[q, my_block],
            send_sem=row_send.at[q],
            recv_sem=row_recv.at[q],
            device_id=to_id[n, rc],
            device_id_type=MESH,
        )

    def exchange(start, stop):
        @pl.loop(start, stop)
        def _(q):
            first = pl.multiple_of(q * width, width)
            for h in range(2):
                source = tok[4 * h : 4 * h + 4, :, pl.ds(first, width)].reshape(4 * TOK, width)
                picked = dot(select[h].reshape(BLOCKS * quad, 4 * TOK), source).astype(BF16)
                picked = picked.reshape(BLOCKS, quad, width)
                stage[q, :, h * quad : (h + 1) * quad, :] = picked
                recv[q, my_block, h * quad : (h + 1) * quad, :] = picked[0]
            for n, rc in order:
                row_copy(q, n, rc).start()

    complete(0)
    ready = [p[0] * LANE // width for p in parts] + [chunks]
    exchange(ready[0], ready[1])

    for n, rc in order:
        b = from_block[n, rc]
        pltpu.make_async_copy(gate_in.at[b], gate_in.at[b], gate_recv.at[b]).wait()
    gates_all = gate_in[...].reshape(BLOCKS * SEATS, TOK)
    counts_all = dot(ones_where(gates_all > 0.0), earlier).astype(BF16)
    gates_all = gates_all.astype(BF16)
    @pl.loop(0, BLOCKS)
    def _(b):
        hit, gates, _ = expand(b * SEATS, gates_all, counts_all)
        column = jnp.sum(jnp.where(hit, gates, 0.0), axis=1, keepdims=True)
        gcol[b] = jnp.broadcast_to(column, (ROWS, LANE))

    complete(1)
    exchange(ready[1], ready[2])
    complete(2)
    exchange(ready[2], ready[3])

    line = iota((LANE, TOK), 0)
    chips = []
    for d in range(3):
        s = (line >> (4 + d)) & 1
        p = pair(k, chip[d])
        v = (1 - k) * (2 * p + s) + k * (2 * s + ((s + p) & 1))
        n = (line >> (1 + d)) & 1
        across = (1 - k) * (3 - v) + k * (v + 1 - 2 * (v & 1))
        chips.append(n * across + (1 - n) * v)
    x, y, z = chips
    other = line & 1
    core = other * (1 - k) + (1 - other) * k
    expert = ((x >> 1) * 16 + z * 4 + y) * 4 + (x & 1) * 2 + core
    owner[...] = expert
    any_named = expert == routes_ref[0:1, :]
    for c in range(1, TOP):
        any_named = any_named | (expert == routes_ref[c : c + 1, :])
    count[...] = dot(ones_where(any_named), earlier)

    back[...] = jnp.zeros_like(back)
    load_weight.wait()

    def down_copy(q, slot):
        first = pl.multiple_of(q * width, width)
        return pltpu.make_async_copy(
            down.at[slot], grad_down_ref.at[:, pl.ds(first, width)], down_sem.at[slot]
        )

    some = BLOCKS // 2

    def project(q):
        first = pl.multiple_of(q * width, width)
        all_rows = recv.at[q, pl.ds(0, BLOCKS - 1)]
        pltpu.make_async_copy(all_rows, all_rows, row_recv.at[q]).wait()

        @pl.loop(0, 2)
        def _(i):
            got = recv[q, pl.ds(i * some, some)].reshape(some * ROWS, width)
            back[pl.ds(i * some, some)] += dot(
                got, weight[:, pl.ds(first, width)], ((1,), (1,))
            ).reshape(some, ROWS, ffe)

    def weight_grad(q, slot):
        @pl.loop(0, BLOCKS)
        def _(b):
            wide = jnp.concatenate([gcol[b]] * (width // LANE), axis=1)
            scaled[pl.ds(b * ROWS, ROWS), :] = (recv[q, b].astype(F32) * wide).astype(BF16)

        down[slot] = dot(hid_t[...], scaled[...]).astype(BF16)
        down_copy(q, slot).start()

    @pl.loop(0, chunks - 1)
    def _(q):
        slot = odd(q)
        project(q)

        @pl.when(q >= 2)
        def _():
            down_copy(q - 2, slot).wait()

        weight_grad(q, slot)

    project(chunks - 1)

    @pl.loop(0, BLOCKS)
    def _(b):
        slots = hid_k[pl.ds(b * ROWS, ROWS), :].astype(F32) * back[b]
        slots = jnp.sum(slots, axis=1, keepdims=True)
        row = iota((ROWS, LANE), 0)
        lane = row + 4 * ((row * 171) >> 11)
        line = jnp.sum(jnp.where(iota((ROWS, LANE), 1) == lane, slots, 0.0), axis=0, keepdims=True)
        sg_out[b] = jnp.broadcast_to(line, (8, LANE))

    def slot_copy(n, rc):
        d = n * 2 + rc
        b = from_block[n, rc]
        return pltpu.make_async_remote_copy(
            src_ref=sg_out.at[b],
            dst_ref=sg_in.at[d],
            send_sem=sg_send.at[d],
            recv_sem=sg_recv.at[d],
            device_id=from_id[n, rc],
            device_id_type=MESH,
        )

    for n, rc in order:
        slot_copy(n, rc).start()
    sg_in[0] = sg_out[my_block]

    last = (chunks - 1) % 2
    down_copy(chunks - 3, last).wait()
    weight_grad(chunks - 1, last)

    for n, rc in order:
        slot_copy(n, rc).wait_recv()
    for d in range(BLOCKS):
        sg_pack[d : d + 1, :] = sg_in[d, 0:1, :]

    def return_copy(f):
        return pltpu.make_async_remote_copy(
            src_ref=sg_pack,
            dst_ref=sg_all.at[mine],
            send_sem=ret_send.at[f],
            recv_sem=ret_recv.at[f],
            device_id=member_id[f],
            device_id_type=MESH,
        )

    for f in range(1, 8):
        return_copy(f).start()
    sg_all[mine] = sg_pack[...]

    for kk in range(2):

        @pl.loop(0, 4)
        def _(i):
            for px in range(2):
                b = kk * 8 + px + 2 * i
                wide = jnp.concatenate([gcol[b]] * (ffe // LANE), axis=1)
                total = back[b] * wide
                for m in range(SEATS):
                    x, y, z = (
                        (s + 2 * p) if kk == 0 else (p + s * (3 - 2 * p))
                        for p, s in zip((px, odd(i), half(i)), (m & 1, (m >> 1) & 1, m >> 2))
                    )
                    first = CAP * ((x % 2) * 2 + kk)
                    natural[(x // 2) * 16 + z * 4 + y, first : first + CAP, :] = total[
                        m * CAP : (m + 1) * CAP
                    ]

    hid[...] = natural[...].reshape(DEV * CAP, ffe).astype(BF16)
    store_hidden = pltpu.make_async_copy(hid, grad_hidden_ref, hid_sem.at[0])
    store_hidden.start()

    for p in range(3):
        for h in range(3):
            for c in range(1 << h):
                rep_copy(p, h, c).wait_send()
    for n, rc in order:
        gate_copy(n, rc).wait_send()
        slot_copy(n, rc).wait_send()

    @pl.loop(0, chunks)
    def _(q):
        all_rows = stage.at[q, pl.ds(1, BLOCKS - 1)]
        pltpu.make_async_copy(all_rows, all_rows, row_send.at[q]).wait()

    for f in range(1, 8):
        table_copy(f).wait_send()
        return_copy(f).wait_send()

    for f in range(1, 8):
        return_copy(f).wait_recv()
    values = pltpu.roll(sg_all[...].reshape(LANE, LANE), LANE - 16 * mine, 1)
    value = jnp.zeros((LANE, TOK), F32)
    for j in range(CAP):
        value = value + jnp.where(count[...] == float(j), values[:, j : j + 1], 0.0)
    for c in range(TOP):
        named = owner[...] == routes_ref[c : c + 1, :]
        grad_gates_ref[c : c + 1, :] = jnp.sum(jnp.where(named, value, 0.0), axis=0, keepdims=True)

    down_copy(chunks - 2, 1 - last).wait()
    down_copy(chunks - 1, last).wait()
    store_hidden.wait()


def finish(hidden_ref, down_ref, grad_hidden_ref, grad_down_ref, hidden, down, sems):
    pieces = 6
    loads, stores = [], []
    for source, held, target in (
        (down_ref, down, grad_down_ref),
        (hidden_ref, hidden, grad_hidden_ref),
    ):
        rows = source.shape[0] // pieces
        for i in range(pieces):
            at = pl.ds(i * rows, rows)
            n = len(loads)
            loads.append(pltpu.make_async_copy(source.at[at], held.at[at], sems.at[0, n]))
            stores.append(pltpu.make_async_copy(held.at[at], target.at[at], sems.at[1, n]))
            loads[-1].start()
    for load, store in zip(loads, stores):
        load.wait()
        store.start()
    for store in stores:
        store.wait()


def local(routes, gate_values, grad_out, hidden, w_down):
    model = grad_out.shape[1]
    ffe = hidden.shape[2]
    slots = DEV * CAP
    width = 256
    chunks = model // width
    kernel_row = jnp.asarray(np.tile(np.argsort(row_orders())[None], (8, 1)), jnp.int32)
    vmem = pl.BlockSpec(memory_space=pltpu.VMEM)
    hbm = pl.BlockSpec(memory_space=pl.ANY)
    dma = pltpu.SemaphoreType.DMA

    def body(*refs):
        kernel(chunks, *refs)

    grad_gates, grad_hidden, grad_down = pl.pallas_call(
        body,
        out_shape=(
            jax.ShapeDtypeStruct((TOP, TOK), F32),
            jax.ShapeDtypeStruct((slots, ffe), BF16),
            jax.ShapeDtypeStruct((ffe, model), BF16),
        ),
        in_specs=[vmem] * 3 + [hbm] * 3,
        out_specs=(vmem, hbm, hbm),
        scratch_shapes=[
            pltpu.VMEM((SEATS, TOK, model), BF16),
            pltpu.VMEM((chunks, BLOCKS, ROWS, width), BF16),
            pltpu.VMEM((chunks, BLOCKS, ROWS, width), BF16),
            pltpu.VMEM((ffe, model), BF16),
            pltpu.VMEM((slots, ffe), BF16),
            pltpu.VMEM((slots, ffe), BF16),
            pltpu.VMEM((ffe, slots), BF16),
            pltpu.VMEM((BLOCKS, ROWS, ffe), F32),
            pltpu.VMEM((DEV // 4, 4 * CAP, ffe), F32),
            pltpu.VMEM((BLOCKS, ROWS, LANE), F32),
            pltpu.VMEM((2, BLOCKS, ROWS // 2, 4 * TOK), BF16),
            pltpu.VMEM((SEATS, DEV, TOK), BF16),
            pltpu.VMEM((SEATS, DEV, TOK), F32),
            pltpu.VMEM((BLOCKS, SEATS, TOK), F32),
            pltpu.VMEM((BLOCKS, SEATS, TOK), F32),
            pltpu.VMEM((slots, width), BF16),
            pltpu.VMEM((2, ffe, width), BF16),
            pltpu.VMEM((BLOCKS, 8, LANE), F32),
            pltpu.VMEM((BLOCKS, 8, LANE), F32),
            pltpu.VMEM((BLOCKS, LANE), F32),
            pltpu.VMEM((SEATS, BLOCKS, LANE), F32),
            pltpu.VMEM((LANE, TOK), jnp.int32),
            pltpu.VMEM((LANE, TOK), F32),
            dma((3,)),
            dma((8,)),
            dma((8,)),
            dma((21,)),
            dma((21,)),
            dma((chunks,)),
            dma((chunks,)),
            dma((BLOCKS,)),
            dma((BLOCKS,)),
            dma((BLOCKS,)),
            dma((BLOCKS,)),
            dma((8,)),
            dma((8,)),
            dma((2,)),
            dma((1,)),
        ],
        compiler_params=pltpu.CompilerParams(
            collective_id=0, has_side_effects=True, vmem_limit_bytes=63 * 1024 * 1024
        ),
        cost_estimate=pl.CostEstimate(
            flops=4 * slots * ffe * model, bytes_accessed=20_000_000, transcendentals=0
        ),
    )(routes.T, gate_values.T, kernel_row, grad_out, hidden[0], w_down[0])

    grad_hidden, grad_down = pl.pallas_call(
        finish,
        out_shape=(
            jax.ShapeDtypeStruct((slots, ffe), BF16),
            jax.ShapeDtypeStruct((ffe, model), BF16),
        ),
        in_specs=[hbm, hbm],
        out_specs=(hbm, hbm),
        scratch_shapes=[
            pltpu.VMEM((slots, ffe), BF16),
            pltpu.VMEM((ffe, model), BF16),
            dma((2, 12)),
        ],
        compiler_params=pltpu.CompilerParams(vmem_limit_bytes=63 * 1024 * 1024),
        cost_estimate=pl.CostEstimate(
            flops=0, bytes_accessed=17_000_000, transcendentals=0
        ),
    )(grad_hidden, grad_down)
    return grad_gates.T, grad_hidden[None], grad_down[None]


def solution(mesh):
    both = ("dp", "tensor")
    in_specs = (P(both, None), P(both, None), P(both, None), P(both, None, None), P(both, None, None))
    out_specs = (P(both, None), P(both, None, None), P(both, None, None))
    return jax.shard_map(local, mesh=mesh, in_specs=in_specs, out_specs=out_specs, check_vma=False)
```

```python
import itertools

import jax
import jax.numpy as jnp
import numpy as np
from jax import lax
from jax.experimental import pallas as pl
from jax.experimental.pallas import tpu as pltpu
from jax.sharding import PartitionSpec as P

MESH = pl.DeviceIdType.MESH
F32 = jnp.float32
BF16 = jnp.bfloat16

DEV = 128
TOK = 128
CAP = 12
TOP = 8
LANE = 128
SEATS = 8
BLOCKS = 16
ROWS = SEATS * CAP


def half(v):
    return lax.div(v, 2)


def odd(v):
    return lax.rem(v, 2)


def near(k, v):
    return (1 - k) * (v + 1 - 2 * odd(v)) + k * (3 - v)


def far(k, v):
    return (1 - k) * (3 - v) + k * (v + 1 - 2 * odd(v))


def seat(k, v):
    return (1 - k) * odd(v) + k * half(v)


def pair(k, v):
    return (1 - k) * half(v) + k * odd(v + half(v))


def place(chip, core):
    x, y, z = chip
    return half(x) * 16 + z * 4 + y, odd(x) * 2 + core


def number(chip, core):
    dp, tensor = place(chip, core)
    return dp * 4 + tensor


def reach(k, chip, n):
    return tuple(far(k, v) if (n >> d) & 1 else v for d, v in enumerate(chip))


def block_of(k, chip, n):
    total = k * 8
    for d, v in enumerate(chip):
        own = pair(k, v)
        total = total + (1 << d) * ((1 - own) if (n >> d) & 1 else own)
    return total


def row_orders():
    natural = np.zeros(DEV * CAP, np.int32)
    for k, b, m in itertools.product(range(2), range(8), range(8)):
        chip = []
        for d in range(3):
            p, s = (b >> d) & 1, (m >> d) & 1
            chip.append((2 * p + s) if k == 0 else (2 * s + (p ^ s)))
        x, y, z = chip
        device = ((x // 2) * 16 + z * 4 + y) * 4 + (x % 2) * 2 + k
        first = ((k * 8 + b) * 8 + m) * CAP
        natural[first : first + CAP] = device * CAP + np.arange(CAP)
    return natural


def iota(shape, dim):
    return lax.broadcasted_iota(jnp.int32, shape, dim)


def dot(a, b, dims=((1,), (0,))):
    return lax.dot_general(a, b, (dims, ((), ())), preferred_element_type=F32)


def ones_where(mask):
    return jnp.where(mask, 1.0, 0.0).astype(BF16)


def expand(first, gates_all, counts_all):
    row = iota((ROWS, LANE), 0)
    of = (row * 171) >> 11
    slot = (row - of * CAP).astype(F32)
    pick = ones_where(iota((ROWS, LANE), 1) == of + first)
    gates = dot(pick, gates_all)
    counts = dot(pick, counts_all)
    hit = (counts == slot) & (gates > 0.0)
    return hit, gates, of


def kernel(
    chunks,
    routes_ref,
    gates_ref,
    kernel_row_ref,
    grad_ref,
    hidden_ref,
    weight_ref,
    grad_gates_ref,
    grad_hidden_ref,
    grad_down_ref,
    tok,
    stage,
    recv,
    weight,
    hid,
    hid_k,
    hid_t,
    back,
    natural,
    gcol,
    select,
    tables,
    gate_f,
    gate_out,
    gate_in,
    scaled,
    down,
    sg_out,
    sg_in,
    sg_pack,
    sg_all,
    owner,
    count,
    in_sem,
    far_sem,
    tab_send,
    tab_recv,
    rep_send,
    rep_recv,
    row_send,
    row_recv,
    gate_send,
    gate_recv,
    sg_send,
    sg_recv,
    ret_send,
    ret_recv,
    down_sem,
    hid_sem,
):
    width = recv.shape[3]
    model = weight.shape[1]
    ffe = weight.shape[0]
    dp = lax.axis_index("dp")
    tensor = lax.axis_index("tensor")
    k = odd(tensor)
    chip = (half(tensor) + 2 * lax.div(dp, 16), lax.rem(dp, 4), lax.rem(lax.div(dp, 4), 4))
    seats = tuple(seat(k, v) for v in chip)
    mine = seats[0] + 2 * seats[1] + 4 * seats[2]
    my_block = block_of(k, chip, 0)
    cores = (k, 1 - k)
    order = [(n, rc) for rc in (0, 1) for n in (7, 3, 5, 6, 1, 2, 4, 0) if (n, rc) != (0, 0)]

    def receiver(n, rc):
        return reach(k, chip, n), cores[rc]

    def sender(n, rc):
        return reach(cores[rc], chip, n), cores[rc]

    def member(flips):
        return tuple(near(k, v) if (flips >> d) & 1 else v for d, v in enumerate(chip))

    to_id = {key: place(*receiver(*key)) for key in order}
    from_id = {key: place(*sender(*key)) for key in order}
    from_block = {(n, rc): block_of(cores[rc], chip, n) for n, rc in order}
    member_id = {f: place(member(f), k) for f in range(1, 8)}

    load_rows = pltpu.make_async_copy(grad_ref, tok.at[mine], in_sem.at[0])
    load_rows.start()
    load_hidden = pltpu.make_async_copy(hidden_ref, hid, in_sem.at[1])
    load_hidden.start()
    load_weight = pltpu.make_async_copy(weight_ref, weight, in_sem.at[2])
    load_weight.start()

    barrier = pltpu.get_barrier_semaphore()
    greet = [member_id[1 << d] for d in range(3)] + [to_id[1 << d, 0] for d in range(3)]
    greet += [to_id[0, 1]]
    for who in greet:
        pl.semaphore_signal(barrier, inc=1, device_id=who, device_id_type=MESH)

    gates_t = gates_ref[...].astype(F32)
    table = jnp.zeros((DEV, TOK), F32)
    for c in range(TOP):
        named = iota((DEV, TOK), 0) == routes_ref[c : c + 1, :]
        table = table + jnp.where(named, gates_t[c : c + 1, :], 0.0)
    tables[mine] = table.astype(BF16)
    load_rows.wait()
    pl.semaphore_wait(barrier, len(greet))

    def tell(d):
        pl.semaphore_signal(
            far_sem.at[d], inc=1, device_id=to_id[1 << d, 0], device_id_type=MESH
        )

    def hear(d):
        pl.semaphore_wait(far_sem.at[d], 1)

    def flipped(flips):
        return sum((1 << d) * ((1 - seats[d]) if flips[d] else seats[d]) for d in range(3))

    def table_copies(h):
        copies = []
        for c in range(1 << h):
            ref = tables.at[flipped([d < h and (c >> d) & 1 for d in range(3)])]
            at = (1 << h) - 1 + c
            copies.append(
                pltpu.make_async_remote_copy(
                    src_ref=ref,
                    dst_ref=ref,
                    send_sem=tab_send.at[at],
                    recv_sem=tab_recv.at[at],
                    device_id=member_id[1 << h],
                    device_id_type=MESH,
                )
            )
        return copies

    def send_tables(h):
        for copy in table_copies(h):
            copy.start()

    def get_tables(h):
        for copy in table_copies(h):
            copy.wait_recv()

    tiles = (6, 5, 5, 5, 6, model // LANE - 27)
    starts = [sum(tiles[:p]) for p in range(7)]
    groups = (range(0, 3), range(3, 6))

    def rep_copy(p, h, c):
        hops = [(d - p) % 3 for d in range(3)]
        slot = flipped([hop < h and (c >> hop) & 1 for hop in hops])
        at = p * 7 + (1 << h) - 1 + c
        ref = tok.at[slot, :, pl.ds(starts[p] * LANE, tiles[p] * LANE)]
        return pltpu.make_async_remote_copy(
            src_ref=ref,
            dst_ref=ref,
            send_sem=rep_send.at[at],
            recv_sem=rep_recv.at[at],
            device_id=member_id[1 << ((p + h) % 3)],
            device_id_type=MESH,
        )

    def own(group):
        for h in range(3):
            for p in group:
                rep_copy(p, h, 0).start()

    def forward_first(group):
        for p in group:
            rep_copy(p, 0, 0).wait_recv()
            rep_copy(p, 1, 1).start()
        for p in group:
            rep_copy(p, 2, 1).start()
            rep_copy(p, 1, 0).wait_recv()
            rep_copy(p, 2, 2).start()

    def forward_last(group):
        for p in group:
            rep_copy(p, 1, 1).wait_recv()
            rep_copy(p, 2, 3).start()

    def complete(group):
        for p in group:
            for c in range(4):
                rep_copy(p, 2, c).wait_recv()

    span = 2 * LANE

    def permute_hidden(start, stop):
        @pl.loop(start, stop)
        def _(i):
            first = pl.multiple_of(i * span, span)
            move = ones_where(kernel_row_ref[0:1, :] == iota((span, DEV * CAP), 0) + first)
            moved = dot(move, hid[...])
            hid_k[pl.ds(first, span), :] = moved.astype(BF16)
            hid_t[:, pl.ds(first, span)] = moved.T.astype(BF16)

    send_tables(0)
    tell(0)
    own(groups[0])
    own(groups[1])
    load_hidden.wait()
    permute_hidden(0, 1)
    get_tables(0)
    send_tables(1)
    hear(0)
    tell(1)
    permute_hidden(1, 2)
    forward_first(groups[0])
    get_tables(1)
    send_tables(2)
    hear(1)
    tell(2)
    permute_hidden(2, 4)
    get_tables(2)
    hear(2)

    gate_f[...] = tables[...].astype(F32)
    for n in range(8):
        for rc in range(2):
            expert = number(*receiver(n, rc))
            for m in range(SEATS):
                gate_out[n * 2 + rc, m : m + 1, :] = gate_f[m, pl.ds(expert, 1), :]
    gate_in[my_block] = gate_out[0]

    def gate_copy(n, rc):
        d = n * 2 + rc
        return pltpu.make_async_remote_copy(
            src_ref=gate_out.at[d],
            dst_ref=gate_in.at[my_block],
            send_sem=gate_send.at[d],
            recv_sem=gate_recv.at[my_block],
            device_id=to_id[n, rc],
            device_id_type=MESH,
        )

    for n, rc in order:
        gate_copy(n, rc).start()

    forward_last(groups[0])
    forward_first(groups[1])

    earlier = ones_where(iota((TOK, TOK), 0) < iota((TOK, TOK), 1))
    gates_all = gate_out[...].reshape(BLOCKS * SEATS, TOK)
    counts_all = dot(ones_where(gates_all > 0.0), earlier).astype(BF16)
    gates_all = gates_all.astype(BF16)
    quad = ROWS // 2

    @pl.loop(0, BLOCKS)
    def _(d):
        hit, _, of = expand(d * SEATS, gates_all, counts_all)
        for h in range(2):
            rows = slice(h * quad, (h + 1) * quad)
            for m in range(4):
                chosen = hit[rows] & (of[rows] == 4 * h + m)
                select[h, d, :, m * TOK : (m + 1) * TOK] = ones_where(chosen)

    def row_copy(q, n, rc):
        d = n * 2 + rc
        return pltpu.make_async_remote_copy(
            src_ref=stage.at[q, d],
            dst_ref=recv.at[q, my_block],
            send_sem=row_send.at[q],
            recv_sem=row_recv.at[q],
            device_id=to_id[n, rc],
            device_id_type=MESH,
        )

    def exchange(start, stop):
        @pl.loop(start, stop)
        def _(q):
            first = pl.multiple_of(q * width, width)
            for h in range(2):
                source = tok[4 * h : 4 * h + 4, :, pl.ds(first, width)].reshape(4 * TOK, width)
                picked = dot(select[h].reshape(BLOCKS * quad, 4 * TOK), source).astype(BF16)
                picked = picked.reshape(BLOCKS, quad, width)
                stage[q, :, h * quad : (h + 1) * quad, :] = picked
                recv[q, my_block, h * quad : (h + 1) * quad, :] = picked[0]
            for n, rc in order:
                row_copy(q, n, rc).start()

    complete(groups[0])
    exchange(0, 3)
    forward_last(groups[1])
    exchange(3, chunks // 2)
    permute_hidden(4, 6)

    for n, rc in order:
        b = from_block[n, rc]
        pltpu.make_async_copy(gate_in.at[b], gate_in.at[b], gate_recv.at[b]).wait()
    gates_all = gate_in[...].reshape(BLOCKS * SEATS, TOK)
    counts_all = dot(ones_where(gates_all > 0.0), earlier).astype(BF16)
    gates_all = gates_all.astype(BF16)
    @pl.loop(0, BLOCKS)
    def _(b):
        hit, gates, _ = expand(b * SEATS, gates_all, counts_all)
        column = jnp.sum(jnp.where(hit, gates, 0.0), axis=1, keepdims=True)
        gcol[b] = jnp.broadcast_to(column, (ROWS, LANE))

    complete(groups[1])
    exchange(chunks // 2, chunks)

    line = iota((LANE, TOK), 0)
    chips = []
    for d in range(3):
        s = (line >> (4 + d)) & 1
        p = pair(k, chip[d])
        v = (1 - k) * (2 * p + s) + k * (2 * s + ((s + p) & 1))
        n = (line >> (1 + d)) & 1
        across = (1 - k) * (3 - v) + k * (v + 1 - 2 * (v & 1))
        chips.append(n * across + (1 - n) * v)
    x, y, z = chips
    other = line & 1
    core = other * (1 - k) + (1 - other) * k
    expert = ((x >> 1) * 16 + z * 4 + y) * 4 + (x & 1) * 2 + core
    owner[...] = expert
    any_named = expert == routes_ref[0:1, :]
    for c in range(1, TOP):
        any_named = any_named | (expert == routes_ref[c : c + 1, :])
    count[...] = dot(ones_where(any_named), earlier)

    back[...] = jnp.zeros_like(back)
    load_weight.wait()

    def down_copy(q, slot):
        first = pl.multiple_of(q * width, width)
        return pltpu.make_async_copy(
            down.at[slot], grad_down_ref.at[:, pl.ds(first, width)], down_sem.at[slot]
        )

    some = BLOCKS // 2

    def arrive(q):
        all_rows = recv.at[q, pl.ds(0, BLOCKS - 1)]
        pltpu.make_async_copy(all_rows, all_rows, row_recv.at[q]).wait()

    def projected(q, i):
        first = pl.multiple_of(q * width, width)
        got = recv[q, pl.ds(i * some, some)].reshape(some * ROWS, width)
        new = dot(got, weight[:, pl.ds(first, width)], ((1,), (1,)))
        return back[pl.ds(i * some, some)] + new.reshape(some, ROWS, ffe)

    def weight_grad(q, slot):
        @pl.loop(0, BLOCKS)
        def _(b):
            wide = jnp.concatenate([gcol[b]] * (width // LANE), axis=1)
            scaled[pl.ds(b * ROWS, ROWS), :] = (recv[q, b].astype(F32) * wide).astype(BF16)

        down[slot] = dot(hid_t[...], scaled[...]).astype(BF16)
        down_copy(q, slot).start()

    @pl.loop(0, chunks - 1)
    def _(q):
        slot = odd(q)
        arrive(q)

        @pl.loop(0, 2)
        def _(i):
            back[pl.ds(i * some, some)] = projected(q, i)

        @pl.when(q >= 2)
        def _():
            down_copy(q - 2, slot).wait()

        weight_grad(q, slot)

    arrive(chunks - 1)

    @pl.loop(0, 2)
    def _(i):
        total = projected(chunks - 1, i)
        back[pl.ds(i * some, some)] = total
        row = iota((ROWS, LANE), 0)
        hit = iota((ROWS, LANE), 1) == row + 4 * ((row * 171) >> 11)
        for j in range(some):
            rows = pl.ds(pl.multiple_of(i * some * ROWS, some * ROWS) + j * ROWS, ROWS)
            slots = jnp.sum(hid_k[rows, :].astype(F32) * total[j], axis=1, keepdims=True)
            line = jnp.sum(jnp.where(hit, slots, 0.0), axis=0, keepdims=True)
            sg_out[i * some + j] = jnp.broadcast_to(line, (8, LANE))

    def slot_copy(n, rc):
        d = n * 2 + rc
        b = from_block[n, rc]
        return pltpu.make_async_remote_copy(
            src_ref=sg_out.at[b],
            dst_ref=sg_in.at[d],
            send_sem=sg_send.at[d],
            recv_sem=sg_recv.at[d],
            device_id=from_id[n, rc],
            device_id_type=MESH,
        )

    for n, rc in order:
        slot_copy(n, rc).start()
    sg_in[0] = sg_out[my_block]

    last = (chunks - 1) % 2
    down_copy(chunks - 3, last).wait()
    weight_grad(chunks - 1, last)

    for n, rc in order:
        slot_copy(n, rc).wait_recv()
    for d in range(BLOCKS):
        sg_pack[d : d + 1, :] = sg_in[d, 0:1, :]

    def return_copy(f):
        return pltpu.make_async_remote_copy(
            src_ref=sg_pack,
            dst_ref=sg_all.at[mine],
            send_sem=ret_send.at[f],
            recv_sem=ret_recv.at[f],
            device_id=member_id[f],
            device_id_type=MESH,
        )

    for f in range(1, 8):
        return_copy(f).start()
    sg_all[mine] = sg_pack[...]

    for kk in range(2):

        @pl.loop(0, 4)
        def _(i):
            for px in range(2):
                b = kk * 8 + px + 2 * i
                wide = jnp.concatenate([gcol[b]] * (ffe // LANE), axis=1)
                total = back[b] * wide
                for m in range(SEATS):
                    x, y, z = (
                        (s + 2 * p) if kk == 0 else (p + s * (3 - 2 * p))
                        for p, s in zip((px, odd(i), half(i)), (m & 1, (m >> 1) & 1, m >> 2))
                    )
                    first = CAP * ((x % 2) * 2 + kk)
                    natural[(x // 2) * 16 + z * 4 + y, first : first + CAP, :] = total[
                        m * CAP : (m + 1) * CAP
                    ]

    hid[...] = natural[...].reshape(DEV * CAP, ffe).astype(BF16)
    store_hidden = pltpu.make_async_copy(hid, grad_hidden_ref, hid_sem.at[0])
    store_hidden.start()

    for p in range(6):
        for h in range(3):
            for c in range(1 << h):
                rep_copy(p, h, c).wait_send()
    for h in range(3):
        for copy in table_copies(h):
            copy.wait_send()
    for n, rc in order:
        gate_copy(n, rc).wait_send()
        slot_copy(n, rc).wait_send()

    @pl.loop(0, chunks)
    def _(q):
        all_rows = stage.at[q, pl.ds(1, BLOCKS - 1)]
        pltpu.make_async_copy(all_rows, all_rows, row_send.at[q]).wait()

    for f in range(1, 8):
        return_copy(f).wait_send()

    for f in range(1, 8):
        return_copy(f).wait_recv()
    values = pltpu.roll(sg_all[...].reshape(LANE, LANE), LANE - 16 * mine, 1)
    value = jnp.zeros((LANE, TOK), F32)
    for j in range(CAP):
        value = value + jnp.where(count[...] == float(j), values[:, j : j + 1], 0.0)
    for c in range(TOP):
        named = owner[...] == routes_ref[c : c + 1, :]
        grad_gates_ref[c : c + 1, :] = jnp.sum(jnp.where(named, value, 0.0), axis=0, keepdims=True)

    down_copy(chunks - 2, 1 - last).wait()
    down_copy(chunks - 1, last).wait()
    store_hidden.wait()


def finish(
    gates_ref,
    hidden_ref,
    down_ref,
    grad_gates_ref,
    grad_hidden_ref,
    grad_down_ref,
    gates,
    hidden,
    down,
    sems,
):
    loads, stores = [], []
    for source, held, target, pieces in (
        (gates_ref, gates, grad_gates_ref, 1),
        (down_ref, down, grad_down_ref, 6),
        (hidden_ref, hidden, grad_hidden_ref, 4),
    ):
        rows = source.shape[0] // pieces
        for i in range(pieces):
            at = pl.ds(i * rows, rows)
            n = len(loads)
            loads.append(pltpu.make_async_copy(source.at[at], held.at[at], sems.at[0, n]))
            stores.append(pltpu.make_async_copy(held.at[at], target.at[at], sems.at[1, n]))
            loads[-1].start()
    for load, store in zip(loads, stores):
        load.wait()
        store.start()
    for store in stores:
        store.wait()


def local(routes, gate_values, grad_out, hidden, w_down):
    model = grad_out.shape[1]
    ffe = hidden.shape[2]
    slots = DEV * CAP
    width = 256
    chunks = model // width
    kernel_row = jnp.asarray(np.tile(np.argsort(row_orders())[None], (8, 1)), jnp.int32)
    vmem = pl.BlockSpec(memory_space=pltpu.VMEM)
    hbm = pl.BlockSpec(memory_space=pl.ANY)
    dma = pltpu.SemaphoreType.DMA

    def body(*refs):
        kernel(chunks, *refs)

    grad_gates, grad_hidden, grad_down = pl.pallas_call(
        body,
        out_shape=(
            jax.ShapeDtypeStruct((TOP, TOK), F32),
            jax.ShapeDtypeStruct((slots, ffe), BF16),
            jax.ShapeDtypeStruct((ffe, model), BF16),
        ),
        in_specs=[vmem] * 3 + [hbm] * 3,
        out_specs=(vmem, hbm, hbm),
        scratch_shapes=[
            pltpu.VMEM((SEATS, TOK, model), BF16),
            pltpu.VMEM((chunks, BLOCKS, ROWS, width), BF16),
            pltpu.VMEM((chunks, BLOCKS, ROWS, width), BF16),
            pltpu.VMEM((ffe, model), BF16),
            pltpu.VMEM((slots, ffe), BF16),
            pltpu.VMEM((slots, ffe), BF16),
            pltpu.VMEM((ffe, slots), BF16),
            pltpu.VMEM((BLOCKS, ROWS, ffe), F32),
            pltpu.VMEM((DEV // 4, 4 * CAP, ffe), F32),
            pltpu.VMEM((BLOCKS, ROWS, LANE), F32),
            pltpu.VMEM((2, BLOCKS, ROWS // 2, 4 * TOK), BF16),
            pltpu.VMEM((SEATS, DEV, TOK), BF16),
            pltpu.VMEM((SEATS, DEV, TOK), F32),
            pltpu.VMEM((BLOCKS, SEATS, TOK), F32),
            pltpu.VMEM((BLOCKS, SEATS, TOK), F32),
            pltpu.VMEM((slots, width), BF16),
            pltpu.VMEM((2, ffe, width), BF16),
            pltpu.VMEM((BLOCKS, 8, LANE), F32),
            pltpu.VMEM((BLOCKS, 8, LANE), F32),
            pltpu.VMEM((BLOCKS, LANE), F32),
            pltpu.VMEM((SEATS, BLOCKS, LANE), F32),
            pltpu.VMEM((LANE, TOK), jnp.int32),
            pltpu.VMEM((LANE, TOK), F32),
            dma((3,)),
            pltpu.SemaphoreType.REGULAR((3,)),
            dma((8,)),
            dma((8,)),
            dma((42,)),
            dma((42,)),
            dma((chunks,)),
            dma((chunks,)),
            dma((BLOCKS,)),
            dma((BLOCKS,)),
            dma((BLOCKS,)),
            dma((BLOCKS,)),
            dma((8,)),
            dma((8,)),
            dma((2,)),
            dma((1,)),
        ],
        compiler_params=pltpu.CompilerParams(
            collective_id=0, has_side_effects=True, vmem_limit_bytes=63 * 1024 * 1024
        ),
        cost_estimate=pl.CostEstimate(
            flops=4 * slots * ffe * model, bytes_accessed=20_000_000, transcendentals=0
        ),
    )(routes.T, gate_values.T, kernel_row, grad_out, hidden[0], w_down[0])

    grad_gates, grad_hidden, grad_down = pl.pallas_call(
        finish,
        out_shape=(
            jax.ShapeDtypeStruct((TOP, TOK), F32),
            jax.ShapeDtypeStruct((slots, ffe), BF16),
            jax.ShapeDtypeStruct((ffe, model), BF16),
        ),
        in_specs=[hbm, hbm, hbm],
        out_specs=(hbm, hbm, hbm),
        scratch_shapes=[
            pltpu.VMEM((TOP, TOK), F32),
            pltpu.VMEM((slots, ffe), BF16),
            pltpu.VMEM((ffe, model), BF16),
            dma((2, 12)),
        ],
        compiler_params=pltpu.CompilerParams(vmem_limit_bytes=63 * 1024 * 1024),
        cost_estimate=pl.CostEstimate(
            flops=0, bytes_accessed=17_000_000, transcendentals=0
        ),
    )(grad_gates, grad_hidden, grad_down)
    return grad_gates.T, grad_hidden[None], grad_down[None]


def solution(mesh):
    both = ("dp", "tensor")
    in_specs = (P(both, None), P(both, None), P(both, None), P(both, None, None), P(both, None, None))
    out_specs = (P(both, None), P(both, None, None), P(both, None, None))
    return jax.shard_map(local, mesh=mesh, in_specs=in_specs, out_specs=out_specs, check_vma=False)
```

```python
import itertools

import jax
import jax.numpy as jnp
import numpy as np
from jax import lax
from jax.experimental import pallas as pl
from jax.experimental.pallas import tpu as pltpu
from jax.sharding import PartitionSpec as P

MESH = pl.DeviceIdType.MESH
F32 = jnp.float32
BF16 = jnp.bfloat16

DEV = 128
TOK = 128
CAP = 12
TOP = 8
LANE = 128
SEATS = 8
BLOCKS = 16
ROWS = SEATS * CAP


def half(v):
    return lax.div(v, 2)


def odd(v):
    return lax.rem(v, 2)


def near(k, v):
    return (1 - k) * (v + 1 - 2 * odd(v)) + k * (3 - v)


def far(k, v):
    return (1 - k) * (3 - v) + k * (v + 1 - 2 * odd(v))


def seat(k, v):
    return (1 - k) * odd(v) + k * half(v)


def pair(k, v):
    return (1 - k) * half(v) + k * odd(v + half(v))


def place(chip, core):
    x, y, z = chip
    return half(x) * 16 + z * 4 + y, odd(x) * 2 + core


def number(chip, core):
    dp, tensor = place(chip, core)
    return dp * 4 + tensor


def reach(k, chip, n):
    return tuple(far(k, v) if (n >> d) & 1 else v for d, v in enumerate(chip))


def block_of(k, chip, n):
    total = k * 8
    for d, v in enumerate(chip):
        own = pair(k, v)
        total = total + (1 << d) * ((1 - own) if (n >> d) & 1 else own)
    return total


def row_orders():
    natural = np.zeros(DEV * CAP, np.int32)
    for k, b, m in itertools.product(range(2), range(8), range(8)):
        chip = []
        for d in range(3):
            p, s = (b >> d) & 1, (m >> d) & 1
            chip.append((2 * p + s) if k == 0 else (2 * s + (p ^ s)))
        x, y, z = chip
        device = ((x // 2) * 16 + z * 4 + y) * 4 + (x % 2) * 2 + k
        first = ((k * 8 + b) * 8 + m) * CAP
        natural[first : first + CAP] = device * CAP + np.arange(CAP)
    return natural


def iota(shape, dim):
    return lax.broadcasted_iota(jnp.int32, shape, dim)


def dot(a, b, dims=((1,), (0,))):
    return lax.dot_general(a, b, (dims, ((), ())), preferred_element_type=F32)


def ones_where(mask):
    return jnp.where(mask, 1.0, 0.0).astype(BF16)


def expand(first, gates_all, counts_all):
    row = iota((ROWS, LANE), 0)
    of = (row * 171) >> 11
    slot = (row - of * CAP).astype(F32)
    pick = ones_where(iota((ROWS, LANE), 1) == of + first)
    gates = dot(pick, gates_all)
    counts = dot(pick, counts_all)
    hit = (counts == slot) & (gates > 0.0)
    return hit, gates, of


def kernel(
    chunks,
    routes_in,
    gates_in,
    kernel_row_in,
    grad_ref,
    hidden_ref,
    weight_ref,
    grad_gates_ref,
    hid,
    weight,
    routes_ref,
    gates_ref,
    kernel_row_ref,
    tok,
    stage,
    recv,
    hid_k,
    hid_t,
    back,
    natural,
    gcol,
    select,
    tables,
    gate_f,
    gate_out,
    gate_in,
    scaled,
    sg_out,
    sg_in,
    sg_pack,
    sg_all,
    owner,
    count,
    in_sem,
    far_sem,
    tab_send,
    tab_recv,
    rep_send,
    rep_recv,
    row_send,
    row_recv,
    gate_send,
    gate_recv,
    sg_send,
    sg_recv,
    ret_send,
    ret_recv,
):
    width = recv.shape[3]
    model = weight.shape[1]
    ffe = weight.shape[0]
    dp = lax.axis_index("dp")
    tensor = lax.axis_index("tensor")
    k = odd(tensor)
    chip = (half(tensor) + 2 * lax.div(dp, 16), lax.rem(dp, 4), lax.rem(lax.div(dp, 4), 4))
    seats = tuple(seat(k, v) for v in chip)
    mine = seats[0] + 2 * seats[1] + 4 * seats[2]
    my_block = block_of(k, chip, 0)
    cores = (k, 1 - k)
    order = [(n, rc) for rc in (0, 1) for n in (7, 3, 5, 6, 1, 2, 4, 0) if (n, rc) != (0, 0)]

    def receiver(n, rc):
        return reach(k, chip, n), cores[rc]

    def sender(n, rc):
        return reach(cores[rc], chip, n), cores[rc]

    def member(flips):
        return tuple(near(k, v) if (flips >> d) & 1 else v for d, v in enumerate(chip))

    to_id = {key: place(*receiver(*key)) for key in order}
    from_id = {key: place(*sender(*key)) for key in order}
    from_block = {(n, rc): block_of(cores[rc], chip, n) for n, rc in order}
    member_id = {f: place(member(f), k) for f in range(1, 8)}

    load_rows = pltpu.make_async_copy(grad_ref, tok.at[mine], in_sem.at[0])
    load_rows.start()
    load_small = [
        pltpu.make_async_copy(routes_in, routes_ref, in_sem.at[3]),
        pltpu.make_async_copy(gates_in, gates_ref, in_sem.at[4]),
        pltpu.make_async_copy(kernel_row_in, kernel_row_ref, in_sem.at[5]),
    ]
    for load in load_small:
        load.start()

    barrier = pltpu.get_barrier_semaphore()
    greet = [member_id[1 << d] for d in range(3)] + [to_id[1 << d, 0] for d in range(3)]
    greet += [to_id[0, 1]]
    for who in greet:
        pl.semaphore_signal(barrier, inc=1, device_id=who, device_id_type=MESH)

    load_hidden = pltpu.make_async_copy(hidden_ref, hid, in_sem.at[1])
    load_hidden.start()
    load_weight = pltpu.make_async_copy(weight_ref, weight, in_sem.at[2])
    load_weight.start()
    for load in load_small:
        load.wait()

    gates_t = gates_ref[...].astype(F32)
    table = jnp.zeros((DEV, TOK), F32)
    for c in range(TOP):
        named = iota((DEV, TOK), 0) == routes_ref[c : c + 1, :]
        table = table + jnp.where(named, gates_t[c : c + 1, :], 0.0)
    tables[mine] = table.astype(BF16)
    load_rows.wait()
    pl.semaphore_wait(barrier, len(greet))

    def tell(d):
        pl.semaphore_signal(
            far_sem.at[d], inc=1, device_id=to_id[1 << d, 0], device_id_type=MESH
        )

    def hear(d):
        pl.semaphore_wait(far_sem.at[d], 1)

    def flipped(flips):
        return sum((1 << d) * ((1 - seats[d]) if flips[d] else seats[d]) for d in range(3))

    def table_copies(h):
        copies = []
        for c in range(1 << h):
            ref = tables.at[flipped([d < h and (c >> d) & 1 for d in range(3)])]
            at = (1 << h) - 1 + c
            copies.append(
                pltpu.make_async_remote_copy(
                    src_ref=ref,
                    dst_ref=ref,
                    send_sem=tab_send.at[at],
                    recv_sem=tab_recv.at[at],
                    device_id=member_id[1 << h],
                    device_id_type=MESH,
                )
            )
        return copies

    def send_tables(h):
        for copy in table_copies(h):
            copy.start()

    def get_tables(h):
        for copy in table_copies(h):
            copy.wait_recv()

    tiles = (6, 5, 5, 5, 6, model // LANE - 27)
    starts = [sum(tiles[:p]) for p in range(7)]
    groups = (range(0, 3), range(3, 6))

    def rep_copy(p, h, c):
        hops = [(d - p) % 3 for d in range(3)]
        slot = flipped([hop < h and (c >> hop) & 1 for hop in hops])
        at = p * 7 + (1 << h) - 1 + c
        ref = tok.at[slot, :, pl.ds(starts[p] * LANE, tiles[p] * LANE)]
        return pltpu.make_async_remote_copy(
            src_ref=ref,
            dst_ref=ref,
            send_sem=rep_send.at[at],
            recv_sem=rep_recv.at[at],
            device_id=member_id[1 << ((p + h) % 3)],
            device_id_type=MESH,
        )

    def own(group):
        for h in range(3):
            for p in group:
                rep_copy(p, h, 0).start()

    def forward_first(group):
        for p in group:
            rep_copy(p, 0, 0).wait_recv()
            rep_copy(p, 1, 1).start()
        for p in group:
            rep_copy(p, 2, 1).start()
            rep_copy(p, 1, 0).wait_recv()
            rep_copy(p, 2, 2).start()

    def forward_last(group):
        for p in group:
            rep_copy(p, 1, 1).wait_recv()
            rep_copy(p, 2, 3).start()

    def complete(group):
        for p in group:
            for c in range(4):
                rep_copy(p, 2, c).wait_recv()

    span = 2 * LANE

    def permute_hidden(start, stop):
        @pl.loop(start, stop)
        def _(i):
            first = pl.multiple_of(i * span, span)
            move = ones_where(kernel_row_ref[0:1, :] == iota((span, DEV * CAP), 0) + first)
            moved = dot(move, hid[...])
            hid_k[pl.ds(first, span), :] = moved.astype(BF16)
            hid_t[:, pl.ds(first, span)] = moved.T.astype(BF16)

    send_tables(0)
    tell(0)
    own(groups[0])
    own(groups[1])
    load_hidden.wait()
    permute_hidden(0, 1)
    get_tables(0)
    send_tables(1)
    hear(0)
    tell(1)
    permute_hidden(1, 2)
    forward_first(groups[0])
    get_tables(1)
    send_tables(2)
    hear(1)
    tell(2)
    permute_hidden(2, 4)
    get_tables(2)
    hear(2)

    gate_f[...] = tables[...].astype(F32)
    for n in range(8):
        for rc in range(2):
            expert = number(*receiver(n, rc))
            for m in range(SEATS):
                gate_out[n * 2 + rc, m : m + 1, :] = gate_f[m, pl.ds(expert, 1), :]
    gate_in[my_block] = gate_out[0]

    def gate_copy(n, rc):
        d = n * 2 + rc
        return pltpu.make_async_remote_copy(
            src_ref=gate_out.at[d],
            dst_ref=gate_in.at[my_block],
            send_sem=gate_send.at[d],
            recv_sem=gate_recv.at[my_block],
            device_id=to_id[n, rc],
            device_id_type=MESH,
        )

    for n, rc in order:
        gate_copy(n, rc).start()

    forward_last(groups[0])
    forward_first(groups[1])

    earlier = ones_where(iota((TOK, TOK), 0) < iota((TOK, TOK), 1))
    gates_all = gate_out[...].reshape(BLOCKS * SEATS, TOK)
    counts_all = dot(ones_where(gates_all > 0.0), earlier).astype(BF16)
    gates_all = gates_all.astype(BF16)
    quad = ROWS // 2

    @pl.loop(0, BLOCKS)
    def _(d):
        hit, _, of = expand(d * SEATS, gates_all, counts_all)
        for h in range(2):
            rows = slice(h * quad, (h + 1) * quad)
            for m in range(4):
                chosen = hit[rows] & (of[rows] == 4 * h + m)
                select[h, d, :, m * TOK : (m + 1) * TOK] = ones_where(chosen)

    def row_copy(q, n, rc):
        d = n * 2 + rc
        return pltpu.make_async_remote_copy(
            src_ref=stage.at[q, d],
            dst_ref=recv.at[q, my_block],
            send_sem=row_send.at[q],
            recv_sem=row_recv.at[q],
            device_id=to_id[n, rc],
            device_id_type=MESH,
        )

    def exchange(start, stop):
        @pl.loop(start, stop)
        def _(q):
            first = pl.multiple_of(q * width, width)
            for h in range(2):
                source = tok[4 * h : 4 * h + 4, :, pl.ds(first, width)].reshape(4 * TOK, width)
                picked = dot(select[h].reshape(BLOCKS * quad, 4 * TOK), source).astype(BF16)
                picked = picked.reshape(BLOCKS, quad, width)
                stage[q, :, h * quad : (h + 1) * quad, :] = picked
                recv[q, my_block, h * quad : (h + 1) * quad, :] = picked[0]
            for n, rc in order:
                row_copy(q, n, rc).start()

    complete(groups[0])
    exchange(0, 3)
    forward_last(groups[1])
    exchange(3, chunks // 2)
    permute_hidden(4, 6)

    for n, rc in order:
        b = from_block[n, rc]
        pltpu.make_async_copy(gate_in.at[b], gate_in.at[b], gate_recv.at[b]).wait()
    gates_all = gate_in[...].reshape(BLOCKS * SEATS, TOK)
    counts_all = dot(ones_where(gates_all > 0.0), earlier).astype(BF16)
    gates_all = gates_all.astype(BF16)
    @pl.loop(0, BLOCKS)
    def _(b):
        hit, gates, _ = expand(b * SEATS, gates_all, counts_all)
        column = jnp.sum(jnp.where(hit, gates, 0.0), axis=1, keepdims=True)
        gcol[b] = jnp.broadcast_to(column, (ROWS, LANE))

    complete(groups[1])
    exchange(chunks // 2, chunks)

    line = iota((LANE, TOK), 0)
    chips = []
    for d in range(3):
        s = (line >> (4 + d)) & 1
        p = pair(k, chip[d])
        v = (1 - k) * (2 * p + s) + k * (2 * s + ((s + p) & 1))
        n = (line >> (1 + d)) & 1
        across = (1 - k) * (3 - v) + k * (v + 1 - 2 * (v & 1))
        chips.append(n * across + (1 - n) * v)
    x, y, z = chips
    other = line & 1
    core = other * (1 - k) + (1 - other) * k
    expert = ((x >> 1) * 16 + z * 4 + y) * 4 + (x & 1) * 2 + core
    owner[...] = expert
    any_named = expert == routes_ref[0:1, :]
    for c in range(1, TOP):
        any_named = any_named | (expert == routes_ref[c : c + 1, :])
    count[...] = dot(ones_where(any_named), earlier)

    back[...] = jnp.zeros_like(back)
    load_weight.wait()

    some = BLOCKS // 2

    def arrive(q):
        all_rows = recv.at[q, pl.ds(0, BLOCKS - 1)]
        pltpu.make_async_copy(all_rows, all_rows, row_recv.at[q]).wait()

    def projected(q, i):
        first = pl.multiple_of(q * width, width)
        got = recv[q, pl.ds(i * some, some)].reshape(some * ROWS, width)
        new = dot(got, weight[:, pl.ds(first, width)], ((1,), (1,)))
        return back[pl.ds(i * some, some)] + new.reshape(some, ROWS, ffe)

    def weight_grad(q):
        first = pl.multiple_of(q * width, width)

        @pl.loop(0, BLOCKS)
        def _(b):
            wide = jnp.concatenate([gcol[b]] * (width // LANE), axis=1)
            scaled[pl.ds(b * ROWS, ROWS), :] = (recv[q, b].astype(F32) * wide).astype(BF16)

        weight[:, pl.ds(first, width)] = dot(hid_t[...], scaled[...]).astype(BF16)

    @pl.loop(0, chunks - 1)
    def _(q):
        arrive(q)

        @pl.loop(0, 2)
        def _(i):
            back[pl.ds(i * some, some)] = projected(q, i)

        weight_grad(q)

    arrive(chunks - 1)

    @pl.loop(0, 2)
    def _(i):
        total = projected(chunks - 1, i)
        back[pl.ds(i * some, some)] = total
        row = iota((ROWS, LANE), 0)
        hit = iota((ROWS, LANE), 1) == row + 4 * ((row * 171) >> 11)
        for j in range(some):
            rows = pl.ds(pl.multiple_of(i * some * ROWS, some * ROWS) + j * ROWS, ROWS)
            slots = jnp.sum(hid_k[rows, :].astype(F32) * total[j], axis=1, keepdims=True)
            line = jnp.sum(jnp.where(hit, slots, 0.0), axis=0, keepdims=True)
            sg_out[i * some + j] = jnp.broadcast_to(line, (8, LANE))

    def slot_copy(n, rc):
        d = n * 2 + rc
        b = from_block[n, rc]
        return pltpu.make_async_remote_copy(
            src_ref=sg_out.at[b],
            dst_ref=sg_in.at[d],
            send_sem=sg_send.at[d],
            recv_sem=sg_recv.at[d],
            device_id=from_id[n, rc],
            device_id_type=MESH,
        )

    for n, rc in order:
        slot_copy(n, rc).start()
    sg_in[0] = sg_out[my_block]

    def order_hidden(kk):
        @pl.loop(0, 4)
        def _(i):
            for px in range(2):
                b = kk * 8 + px + 2 * i
                wide = jnp.concatenate([gcol[b]] * (ffe // LANE), axis=1)
                total = back[b] * wide
                for m in range(SEATS):
                    x, y, z = (
                        (s + 2 * p) if kk == 0 else (p + s * (3 - 2 * p))
                        for p, s in zip((px, odd(i), half(i)), (m & 1, (m >> 1) & 1, m >> 2))
                    )
                    first = CAP * ((x % 2) * 2 + kk)
                    natural[(x // 2) * 16 + z * 4 + y, first : first + CAP, :] = total[
                        m * CAP : (m + 1) * CAP
                    ]

    weight_grad(chunks - 1)
    order_hidden(0)

    for n, rc in order:
        slot_copy(n, rc).wait_recv()
    for d in range(BLOCKS):
        sg_pack[d : d + 1, :] = sg_in[d, 0:1, :]

    def return_copy(f):
        return pltpu.make_async_remote_copy(
            src_ref=sg_pack,
            dst_ref=sg_all.at[mine],
            send_sem=ret_send.at[f],
            recv_sem=ret_recv.at[f],
            device_id=member_id[f],
            device_id_type=MESH,
        )

    for f in range(1, 8):
        return_copy(f).start()
    sg_all[mine] = sg_pack[...]

    order_hidden(1)
    hid[...] = natural[...].reshape(DEV * CAP, ffe).astype(BF16)

    for p in range(6):
        for h in range(3):
            for c in range(1 << h):
                rep_copy(p, h, c).wait_send()
    for h in range(3):
        for copy in table_copies(h):
            copy.wait_send()
    for n, rc in order:
        gate_copy(n, rc).wait_send()
        slot_copy(n, rc).wait_send()

    @pl.loop(0, chunks)
    def _(q):
        all_rows = stage.at[q, pl.ds(1, BLOCKS - 1)]
        pltpu.make_async_copy(all_rows, all_rows, row_send.at[q]).wait()

    for f in range(1, 8):
        return_copy(f).wait_send()

    for f in range(1, 8):
        return_copy(f).wait_recv()
    values = pltpu.roll(sg_all[...].reshape(LANE, LANE), LANE - 16 * mine, 1)
    value = jnp.zeros((LANE, TOK), F32)
    for j in range(CAP):
        value = value + jnp.where(count[...] == float(j), values[:, j : j + 1], 0.0)
    for c in range(TOP):
        named = owner[...] == routes_ref[c : c + 1, :]
        grad_gates_ref[c : c + 1, :] = jnp.sum(jnp.where(named, value, 0.0), axis=0, keepdims=True)


def finish(gates, hidden, down, grad_gates_ref, grad_hidden_ref, grad_down_ref, sems):
    stores = []
    for held, target in ((down, grad_down_ref), (hidden, grad_hidden_ref), (gates, grad_gates_ref)):
        stores.append(pltpu.make_async_copy(held, target, sems.at[len(stores)]))
        stores[-1].start()
    for store in stores:
        store.wait()


def local(routes, gate_values, grad_out, hidden, w_down):
    model = grad_out.shape[1]
    ffe = hidden.shape[2]
    slots = DEV * CAP
    width = 256
    chunks = model // width
    kernel_row = jnp.asarray(np.tile(np.argsort(row_orders())[None], (8, 1)), jnp.int32)
    vmem = pl.BlockSpec(memory_space=pltpu.VMEM)
    hbm = pl.BlockSpec(memory_space=pl.ANY)
    dma = pltpu.SemaphoreType.DMA

    def body(*refs):
        kernel(chunks, *refs)

    grad_gates, grad_hidden, grad_down = pl.pallas_call(
        body,
        out_shape=(
            pltpu.VMEM((TOP, TOK), F32),
            pltpu.VMEM((slots, ffe), BF16),
            pltpu.VMEM((ffe, model), BF16),
        ),
        in_specs=[hbm] * 6,
        out_specs=(vmem, vmem, vmem),
        scratch_shapes=[
            pltpu.VMEM((TOP, TOK), jnp.int32),
            pltpu.VMEM((TOP, TOK), BF16),
            pltpu.VMEM((8, slots), jnp.int32),
            pltpu.VMEM((SEATS, TOK, model), BF16),
            pltpu.VMEM((chunks, BLOCKS, ROWS, width), BF16),
            pltpu.VMEM((chunks, BLOCKS, ROWS, width), BF16),
            pltpu.VMEM((slots, ffe), BF16),
            pltpu.VMEM((ffe, slots), BF16),
            pltpu.VMEM((BLOCKS, ROWS, ffe), F32),
            pltpu.VMEM((DEV // 4, 4 * CAP, ffe), F32),
            pltpu.VMEM((BLOCKS, ROWS, LANE), F32),
            pltpu.VMEM((2, BLOCKS, ROWS // 2, 4 * TOK), BF16),
            pltpu.VMEM((SEATS, DEV, TOK), BF16),
            pltpu.VMEM((SEATS, DEV, TOK), F32),
            pltpu.VMEM((BLOCKS, SEATS, TOK), F32),
            pltpu.VMEM((BLOCKS, SEATS, TOK), F32),
            pltpu.VMEM((slots, width), BF16),
            pltpu.VMEM((BLOCKS, 8, LANE), F32),
            pltpu.VMEM((BLOCKS, 8, LANE), F32),
            pltpu.VMEM((BLOCKS, LANE), F32),
            pltpu.VMEM((SEATS, BLOCKS, LANE), F32),
            pltpu.VMEM((LANE, TOK), jnp.int32),
            pltpu.VMEM((LANE, TOK), F32),
            dma((6,)),
            pltpu.SemaphoreType.REGULAR((3,)),
            dma((8,)),
            dma((8,)),
            dma((42,)),
            dma((42,)),
            dma((chunks,)),
            dma((chunks,)),
            dma((BLOCKS,)),
            dma((BLOCKS,)),
            dma((BLOCKS,)),
            dma((BLOCKS,)),
            dma((8,)),
            dma((8,)),
        ],
        compiler_params=pltpu.CompilerParams(
            collective_id=0, has_side_effects=True, vmem_limit_bytes=54 * 1024 * 1024
        ),
        cost_estimate=pl.CostEstimate(
            flops=4 * slots * ffe * model, bytes_accessed=20_000_000, transcendentals=0
        ),
    )(routes.T, gate_values.T, kernel_row, grad_out, hidden[0], w_down[0])

    grad_gates, grad_hidden, grad_down = pl.pallas_call(
        finish,
        out_shape=(
            jax.ShapeDtypeStruct((TOP, TOK), F32),
            jax.ShapeDtypeStruct((slots, ffe), BF16),
            jax.ShapeDtypeStruct((ffe, model), BF16),
        ),
        in_specs=[vmem, vmem, vmem],
        out_specs=(hbm, hbm, hbm),
        scratch_shapes=[
            dma((3,)),
        ],
        compiler_params=pltpu.CompilerParams(vmem_limit_bytes=2 * 1024 * 1024),
        cost_estimate=pl.CostEstimate(
            flops=0, bytes_accessed=17_000_000, transcendentals=0
        ),
    )(grad_gates, grad_hidden, grad_down)
    return grad_gates.T, grad_hidden[None], grad_down[None]


def solution(mesh):
    both = ("dp", "tensor")
    in_specs = (P(both, None), P(both, None), P(both, None), P(both, None, None), P(both, None, None))
    out_specs = (P(both, None), P(both, None, None), P(both, None, None))
    return jax.shard_map(local, mesh=mesh, in_specs=in_specs, out_specs=out_specs, check_vma=False)
```

```python
import itertools

import jax
import jax.numpy as jnp
import numpy as np
from jax import lax
from jax.experimental import pallas as pl
from jax.experimental.pallas import tpu as pltpu
from jax.sharding import PartitionSpec as P

MESH = pl.DeviceIdType.MESH
F32 = jnp.float32
BF16 = jnp.bfloat16

DEV = 128
TOK = 128
CAP = 12
TOP = 8
LANE = 128
SEATS = 8
BLOCKS = 16
ROWS = SEATS * CAP


def half(v):
    return lax.div(v, 2)


def odd(v):
    return lax.rem(v, 2)


def near(k, v):
    return (1 - k) * (v + 1 - 2 * odd(v)) + k * (3 - v)


def far(k, v):
    return (1 - k) * (3 - v) + k * (v + 1 - 2 * odd(v))


def seat(k, v):
    return (1 - k) * odd(v) + k * half(v)


def pair(k, v):
    return (1 - k) * half(v) + k * odd(v + half(v))


def place(chip, core):
    x, y, z = chip
    return half(x) * 16 + z * 4 + y, odd(x) * 2 + core


def number(chip, core):
    dp, tensor = place(chip, core)
    return dp * 4 + tensor


def reach(k, chip, n):
    return tuple(far(k, v) if (n >> d) & 1 else v for d, v in enumerate(chip))


def block_of(k, chip, n):
    total = k * 8
    for d, v in enumerate(chip):
        own = pair(k, v)
        total = total + (1 << d) * ((1 - own) if (n >> d) & 1 else own)
    return total


def row_orders():
    natural = np.zeros(DEV * CAP, np.int32)
    for k, b, m in itertools.product(range(2), range(8), range(8)):
        chip = []
        for d in range(3):
            p, s = (b >> d) & 1, (m >> d) & 1
            chip.append((2 * p + s) if k == 0 else (2 * s + (p ^ s)))
        x, y, z = chip
        device = ((x // 2) * 16 + z * 4 + y) * 4 + (x % 2) * 2 + k
        first = ((k * 8 + b) * 8 + m) * CAP
        natural[first : first + CAP] = device * CAP + np.arange(CAP)
    return natural


def iota(shape, dim):
    return lax.broadcasted_iota(jnp.int32, shape, dim)


def dot(a, b, dims=((1,), (0,))):
    return lax.dot_general(a, b, (dims, ((), ())), preferred_element_type=F32)


def ones_where(mask):
    return jnp.where(mask, 1.0, 0.0).astype(BF16)


def expand(first, gates_all, counts_all):
    row = iota((ROWS, LANE), 0)
    of = (row * 171) >> 11
    slot = (row - of * CAP).astype(F32)
    pick = ones_where(iota((ROWS, LANE), 1) == of + first)
    gates = dot(pick, gates_all)
    counts = dot(pick, counts_all)
    hit = (counts == slot) & (gates > 0.0)
    return hit, gates, of


def kernel(
    chunks,
    routes_in,
    gates_in,
    kernel_row_in,
    grad_ref,
    hidden_ref,
    weight_ref,
    grad_gates_ref,
    hid,
    weight,
    routes_ref,
    gates_ref,
    kernel_row_ref,
    tok,
    stage,
    recv,
    hid_k,
    hid_t,
    back,
    natural,
    gcol,
    select,
    tables,
    gate_f,
    gate_out,
    gate_in,
    scaled,
    sg_out,
    sg_in,
    sg_pack,
    sg_all,
    owner,
    count,
    in_sem,
    far_sem,
    tab_send,
    tab_recv,
    rep_send,
    rep_recv,
    row_send,
    row_recv,
    gate_send,
    gate_recv,
    sg_send,
    sg_recv,
    ret_send,
    ret_recv,
):
    width = recv.shape[3]
    model = weight.shape[1]
    ffe = weight.shape[0]
    dp = lax.axis_index("dp")
    tensor = lax.axis_index("tensor")
    k = odd(tensor)
    chip = (half(tensor) + 2 * lax.div(dp, 16), lax.rem(dp, 4), lax.rem(lax.div(dp, 4), 4))
    seats = tuple(seat(k, v) for v in chip)
    mine = seats[0] + 2 * seats[1] + 4 * seats[2]
    my_block = block_of(k, chip, 0)
    cores = (k, 1 - k)
    order = [(n, rc) for rc in (0, 1) for n in (7, 3, 5, 6, 1, 2, 4, 0) if (n, rc) != (0, 0)]

    def receiver(n, rc):
        return reach(k, chip, n), cores[rc]

    def sender(n, rc):
        return reach(cores[rc], chip, n), cores[rc]

    def member(flips):
        return tuple(near(k, v) if (flips >> d) & 1 else v for d, v in enumerate(chip))

    to_id = {key: place(*receiver(*key)) for key in order}
    from_id = {key: place(*sender(*key)) for key in order}
    from_block = {(n, rc): block_of(cores[rc], chip, n) for n, rc in order}
    member_id = {f: place(member(f), k) for f in range(1, 8)}

    load_rows = pltpu.make_async_copy(grad_ref, tok.at[mine], in_sem.at[0])
    load_rows.start()
    load_small = [
        pltpu.make_async_copy(routes_in, routes_ref, in_sem.at[3]),
        pltpu.make_async_copy(gates_in, gates_ref, in_sem.at[4]),
        pltpu.make_async_copy(kernel_row_in, kernel_row_ref, in_sem.at[5]),
    ]
    for load in load_small:
        load.start()

    barrier = pltpu.get_barrier_semaphore()
    greet = [member_id[1 << d] for d in range(3)] + [to_id[1 << d, 0] for d in range(3)]
    greet += [to_id[0, 1]]
    for who in greet:
        pl.semaphore_signal(barrier, inc=1, device_id=who, device_id_type=MESH)

    load_hidden = pltpu.make_async_copy(hidden_ref, hid, in_sem.at[1])
    load_hidden.start()
    load_weight = pltpu.make_async_copy(weight_ref, weight, in_sem.at[2])
    load_weight.start()
    for load in load_small:
        load.wait()

    gates_t = gates_ref[...].astype(F32)
    table = jnp.zeros((DEV, TOK), F32)
    for c in range(TOP):
        named = iota((DEV, TOK), 0) == routes_ref[c : c + 1, :]
        table = table + jnp.where(named, gates_t[c : c + 1, :], 0.0)
    tables[mine] = table.astype(BF16)
    load_rows.wait()
    pl.semaphore_wait(barrier, len(greet))

    def tell(d):
        pl.semaphore_signal(
            far_sem.at[d], inc=1, device_id=to_id[1 << d, 0], device_id_type=MESH
        )

    def hear(d):
        pl.semaphore_wait(far_sem.at[d], 1)

    def flipped(flips):
        return sum((1 << d) * ((1 - seats[d]) if flips[d] else seats[d]) for d in range(3))

    def table_copies(h):
        copies = []
        for c in range(1 << h):
            ref = tables.at[flipped([d < h and (c >> d) & 1 for d in range(3)])]
            at = (1 << h) - 1 + c
            copies.append(
                pltpu.make_async_remote_copy(
                    src_ref=ref,
                    dst_ref=ref,
                    send_sem=tab_send.at[at],
                    recv_sem=tab_recv.at[at],
                    device_id=member_id[1 << h],
                    device_id_type=MESH,
                )
            )
        return copies

    def send_tables(h):
        for copy in table_copies(h):
            copy.start()

    def get_tables(h):
        for copy in table_copies(h):
            copy.wait_recv()

    tiles = (7, 7, 6, 4, 4, model // LANE - 28)
    starts = [sum(tiles[:p]) for p in range(7)]
    groups = (range(0, 3), range(3, 6))

    def rep_copy(p, h, c):
        hops = [(d - p) % 3 for d in range(3)]
        slot = flipped([hop < h and (c >> hop) & 1 for hop in hops])
        at = p * 7 + (1 << h) - 1 + c
        ref = tok.at[slot, :, pl.ds(starts[p] * LANE, tiles[p] * LANE)]
        return pltpu.make_async_remote_copy(
            src_ref=ref,
            dst_ref=ref,
            send_sem=rep_send.at[at],
            recv_sem=rep_recv.at[at],
            device_id=member_id[1 << ((p + h) % 3)],
            device_id_type=MESH,
        )

    def own(group):
        for h in range(3):
            for p in group:
                rep_copy(p, h, 0).start()

    def forward_first(group):
        for p in group:
            rep_copy(p, 0, 0).wait_recv()
            rep_copy(p, 1, 1).start()
        for p in group:
            rep_copy(p, 2, 1).start()
        for p in group:
            rep_copy(p, 1, 0).wait_recv()
            rep_copy(p, 2, 2).start()

    def forward_last(group):
        for p in group:
            rep_copy(p, 1, 1).wait_recv()
            rep_copy(p, 2, 3).start()

    def complete(group):
        for p in group:
            for c in range(4):
                rep_copy(p, 2, c).wait_recv()

    span = 2 * LANE

    def permute_hidden(start, stop):
        @pl.loop(start, stop)
        def _(i):
            first = pl.multiple_of(i * span, span)
            move = ones_where(kernel_row_ref[0:1, :] == iota((span, DEV * CAP), 0) + first)
            moved = dot(move, hid[...])
            hid_k[pl.ds(first, span), :] = moved.astype(BF16)
            hid_t[:, pl.ds(first, span)] = moved.T.astype(BF16)

    send_tables(0)
    tell(0)
    own(groups[0])
    own(groups[1])
    load_hidden.wait()
    permute_hidden(0, 1)
    get_tables(0)
    send_tables(1)
    hear(0)
    tell(1)
    permute_hidden(1, 2)
    forward_first(groups[0])
    get_tables(1)
    send_tables(2)
    hear(1)
    tell(2)
    permute_hidden(2, 4)
    get_tables(2)
    hear(2)

    gate_f[...] = tables[...].astype(F32)
    for n in range(8):
        for rc in range(2):
            expert = number(*receiver(n, rc))
            for m in range(SEATS):
                gate_out[n * 2 + rc, m : m + 1, :] = gate_f[m, pl.ds(expert, 1), :]
    gate_in[my_block] = gate_out[0]

    def gate_copy(n, rc):
        d = n * 2 + rc
        return pltpu.make_async_remote_copy(
            src_ref=gate_out.at[d],
            dst_ref=gate_in.at[my_block],
            send_sem=gate_send.at[d],
            recv_sem=gate_recv.at[my_block],
            device_id=to_id[n, rc],
            device_id_type=MESH,
        )

    for n, rc in order:
        gate_copy(n, rc).start()

    forward_last(groups[0])
    forward_first(groups[1])

    earlier = ones_where(iota((TOK, TOK), 0) < iota((TOK, TOK), 1))
    gates_all = gate_out[...].reshape(BLOCKS * SEATS, TOK)
    counts_all = dot(ones_where(gates_all > 0.0), earlier).astype(BF16)
    gates_all = gates_all.astype(BF16)
    quad = ROWS // 2

    @pl.loop(0, BLOCKS)
    def _(d):
        hit, _, of = expand(d * SEATS, gates_all, counts_all)
        for h in range(2):
            rows = slice(h * quad, (h + 1) * quad)
            for m in range(4):
                chosen = hit[rows] & (of[rows] == 4 * h + m)
                select[h, d, :, m * TOK : (m + 1) * TOK] = ones_where(chosen)

    def row_copy(q, n, rc):
        d = n * 2 + rc
        return pltpu.make_async_remote_copy(
            src_ref=stage.at[q, d],
            dst_ref=recv.at[q, my_block],
            send_sem=row_send.at[q],
            recv_sem=row_recv.at[q],
            device_id=to_id[n, rc],
            device_id_type=MESH,
        )

    def exchange(start, stop):
        @pl.loop(start, stop)
        def _(q):
            first = pl.multiple_of(q * width, width)
            for h in range(2):
                source = tok[4 * h : 4 * h + 4, :, pl.ds(first, width)].reshape(4 * TOK, width)
                picked = dot(select[h].reshape(BLOCKS * quad, 4 * TOK), source).astype(BF16)
                picked = picked.reshape(BLOCKS, quad, width)
                stage[q, :, h * quad : (h + 1) * quad, :] = picked
                recv[q, my_block, h * quad : (h + 1) * quad, :] = picked[0]
            for n, rc in order:
                row_copy(q, n, rc).start()

    complete(groups[0])
    forward_last(groups[1])
    first = starts[3] * LANE // width
    exchange(0, first)
    permute_hidden(4, 6)

    for n, rc in order:
        b = from_block[n, rc]
        pltpu.make_async_copy(gate_in.at[b], gate_in.at[b], gate_recv.at[b]).wait()
    gates_all = gate_in[...].reshape(BLOCKS * SEATS, TOK)
    counts_all = dot(ones_where(gates_all > 0.0), earlier).astype(BF16)
    gates_all = gates_all.astype(BF16)
    @pl.loop(0, BLOCKS)
    def _(b):
        hit, gates, _ = expand(b * SEATS, gates_all, counts_all)
        column = jnp.sum(jnp.where(hit, gates, 0.0), axis=1, keepdims=True)
        gcol[b] = jnp.broadcast_to(column, (ROWS, LANE))

    complete(groups[1])
    exchange(first, chunks)

    line = iota((LANE, TOK), 0)
    chips = []
    for d in range(3):
        s = (line >> (4 + d)) & 1
        p = pair(k, chip[d])
        v = (1 - k) * (2 * p + s) + k * (2 * s + ((s + p) & 1))
        n = (line >> (1 + d)) & 1
        across = (1 - k) * (3 - v) + k * (v + 1 - 2 * (v & 1))
        chips.append(n * across + (1 - n) * v)
    x, y, z = chips
    other = line & 1
    core = other * (1 - k) + (1 - other) * k
    expert = ((x >> 1) * 16 + z * 4 + y) * 4 + (x & 1) * 2 + core
    owner[...] = expert
    any_named = expert == routes_ref[0:1, :]
    for c in range(1, TOP):
        any_named = any_named | (expert == routes_ref[c : c + 1, :])
    count[...] = dot(ones_where(any_named), earlier)

    back[...] = jnp.zeros_like(back)
    load_weight.wait()

    some = BLOCKS // 2

    def arrive(q):
        all_rows = recv.at[q, pl.ds(0, BLOCKS - 1)]
        pltpu.make_async_copy(all_rows, all_rows, row_recv.at[q]).wait()

    def projected(q, i):
        first = pl.multiple_of(q * width, width)
        got = recv[q, pl.ds(i * some, some)].reshape(some * ROWS, width)
        new = dot(got, weight[:, pl.ds(first, width)], ((1,), (1,)))
        return back[pl.ds(i * some, some)] + new.reshape(some, ROWS, ffe)

    def weight_grad(q):
        first = pl.multiple_of(q * width, width)

        @pl.loop(0, BLOCKS)
        def _(b):
            wide = jnp.concatenate([gcol[b]] * (width // LANE), axis=1)
            scaled[pl.ds(b * ROWS, ROWS), :] = (recv[q, b].astype(F32) * wide).astype(BF16)

        weight[:, pl.ds(first, width)] = dot(hid_t[...], scaled[...]).astype(BF16)

    @pl.loop(0, chunks - 1)
    def _(q):
        arrive(q)

        @pl.loop(0, 2)
        def _(i):
            back[pl.ds(i * some, some)] = projected(q, i)

        weight_grad(q)

    arrive(chunks - 1)

    @pl.loop(0, 2)
    def _(i):
        total = projected(chunks - 1, i)
        back[pl.ds(i * some, some)] = total
        row = iota((ROWS, LANE), 0)
        hit = iota((ROWS, LANE), 1) == row + 4 * ((row * 171) >> 11)
        for j in range(some):
            rows = pl.ds(pl.multiple_of(i * some * ROWS, some * ROWS) + j * ROWS, ROWS)
            slots = jnp.sum(hid_k[rows, :].astype(F32) * total[j], axis=1, keepdims=True)
            line = jnp.sum(jnp.where(hit, slots, 0.0), axis=0, keepdims=True)
            sg_out[i * some + j] = jnp.broadcast_to(line, (8, LANE))

    def slot_copy(n, rc):
        d = n * 2 + rc
        b = from_block[n, rc]
        return pltpu.make_async_remote_copy(
            src_ref=sg_out.at[b],
            dst_ref=sg_in.at[d],
            send_sem=sg_send.at[d],
            recv_sem=sg_recv.at[d],
            device_id=from_id[n, rc],
            device_id_type=MESH,
        )

    for n, rc in order:
        slot_copy(n, rc).start()
    sg_in[0] = sg_out[my_block]

    def order_hidden(kk):
        @pl.loop(0, 4)
        def _(i):
            for px in range(2):
                b = kk * 8 + px + 2 * i
                wide = jnp.concatenate([gcol[b]] * (ffe // LANE), axis=1)
                total = back[b] * wide
                for m in range(SEATS):
                    x, y, z = (
                        (s + 2 * p) if kk == 0 else (p + s * (3 - 2 * p))
                        for p, s in zip((px, odd(i), half(i)), (m & 1, (m >> 1) & 1, m >> 2))
                    )
                    first = CAP * ((x % 2) * 2 + kk)
                    natural[(x // 2) * 16 + z * 4 + y, first : first + CAP, :] = total[
                        m * CAP : (m + 1) * CAP
                    ]

    weight_grad(chunks - 1)
    order_hidden(0)

    for n, rc in order:
        slot_copy(n, rc).wait_recv()
    for d in range(BLOCKS):
        sg_pack[d : d + 1, :] = sg_in[d, 0:1, :]

    def return_copy(f):
        return pltpu.make_async_remote_copy(
            src_ref=sg_pack,
            dst_ref=sg_all.at[mine],
            send_sem=ret_send.at[f],
            recv_sem=ret_recv.at[f],
            device_id=member_id[f],
            device_id_type=MESH,
        )

    for f in range(1, 8):
        return_copy(f).start()
    sg_all[mine] = sg_pack[...]

    order_hidden(1)
    hid[...] = natural[...].reshape(DEV * CAP, ffe).astype(BF16)

    for p in range(6):
        for h in range(3):
            for c in range(1 << h):
                rep_copy(p, h, c).wait_send()
    for h in range(3):
        for copy in table_copies(h):
            copy.wait_send()
    for n, rc in order:
        gate_copy(n, rc).wait_send()
        slot_copy(n, rc).wait_send()

    @pl.loop(0, chunks)
    def _(q):
        all_rows = stage.at[q, pl.ds(1, BLOCKS - 1)]
        pltpu.make_async_copy(all_rows, all_rows, row_send.at[q]).wait()

    for f in range(1, 8):
        return_copy(f).wait_send()

    for f in range(1, 8):
        return_copy(f).wait_recv()
    values = pltpu.roll(sg_all[...].reshape(LANE, LANE), LANE - 16 * mine, 1)
    value = jnp.zeros((LANE, TOK), F32)
    for j in range(CAP):
        value = value + jnp.where(count[...] == float(j), values[:, j : j + 1], 0.0)
    for c in range(TOP):
        named = owner[...] == routes_ref[c : c + 1, :]
        grad_gates_ref[c : c + 1, :] = jnp.sum(jnp.where(named, value, 0.0), axis=0, keepdims=True)


def finish(gates, hidden, down, grad_gates_ref, grad_hidden_ref, grad_down_ref, sems):
    stores = []
    for held, target, pieces in (
        (down, grad_down_ref, 8),
        (hidden, grad_hidden_ref, 4),
        (gates, grad_gates_ref, 1),
    ):
        rows = held.shape[0] // pieces
        for i in range(pieces):
            at = pl.ds(i * rows, rows)
            sem = sems.at[len(stores)]
            stores.append(pltpu.make_async_copy(held.at[at], target.at[at], sem))
            stores[-1].start()
    for store in stores:
        store.wait()


def local(routes, gate_values, grad_out, hidden, w_down):
    model = grad_out.shape[1]
    ffe = hidden.shape[2]
    slots = DEV * CAP
    width = 256
    chunks = model // width
    kernel_row = jnp.asarray(np.tile(np.argsort(row_orders())[None], (8, 1)), jnp.int32)
    vmem = pl.BlockSpec(memory_space=pltpu.VMEM)
    hbm = pl.BlockSpec(memory_space=pl.ANY)
    dma = pltpu.SemaphoreType.DMA

    def body(*refs):
        kernel(chunks, *refs)

    grad_gates, grad_hidden, grad_down = pl.pallas_call(
        body,
        out_shape=(
            pltpu.VMEM((TOP, TOK), F32),
            pltpu.VMEM((slots, ffe), BF16),
            pltpu.VMEM((ffe, model), BF16),
        ),
        in_specs=[hbm] * 6,
        out_specs=(vmem, vmem, vmem),
        scratch_shapes=[
            pltpu.VMEM((TOP, TOK), jnp.int32),
            pltpu.VMEM((TOP, TOK), BF16),
            pltpu.VMEM((8, slots), jnp.int32),
            pltpu.VMEM((SEATS, TOK, model), BF16),
            pltpu.VMEM((chunks, BLOCKS, ROWS, width), BF16),
            pltpu.VMEM((chunks, BLOCKS, ROWS, width), BF16),
            pltpu.VMEM((slots, ffe), BF16),
            pltpu.VMEM((ffe, slots), BF16),
            pltpu.VMEM((BLOCKS, ROWS, ffe), F32),
            pltpu.VMEM((DEV // 4, 4 * CAP, ffe), F32),
            pltpu.VMEM((BLOCKS, ROWS, LANE), F32),
            pltpu.VMEM((2, BLOCKS, ROWS // 2, 4 * TOK), BF16),
            pltpu.VMEM((SEATS, DEV, TOK), BF16),
            pltpu.VMEM((SEATS, DEV, TOK), F32),
            pltpu.VMEM((BLOCKS, SEATS, TOK), F32),
            pltpu.VMEM((BLOCKS, SEATS, TOK), F32),
            pltpu.VMEM((slots, width), BF16),
            pltpu.VMEM((BLOCKS, 8, LANE), F32),
            pltpu.VMEM((BLOCKS, 8, LANE), F32),
            pltpu.VMEM((BLOCKS, LANE), F32),
            pltpu.VMEM((SEATS, BLOCKS, LANE), F32),
            pltpu.VMEM((LANE, TOK), jnp.int32),
            pltpu.VMEM((LANE, TOK), F32),
            dma((6,)),
            pltpu.SemaphoreType.REGULAR((3,)),
            dma((8,)),
            dma((8,)),
            dma((42,)),
            dma((42,)),
            dma((chunks,)),
            dma((chunks,)),
            dma((BLOCKS,)),
            dma((BLOCKS,)),
            dma((BLOCKS,)),
            dma((BLOCKS,)),
            dma((8,)),
            dma((8,)),
        ],
        compiler_params=pltpu.CompilerParams(
            collective_id=0, has_side_effects=True, vmem_limit_bytes=54 * 1024 * 1024
        ),
        cost_estimate=pl.CostEstimate(
            flops=4 * slots * ffe * model, bytes_accessed=20_000_000, transcendentals=0
        ),
    )(routes.T, gate_values.T, kernel_row, grad_out, hidden[0], w_down[0])

    grad_gates, grad_hidden, grad_down = pl.pallas_call(
        finish,
        out_shape=(
            jax.ShapeDtypeStruct((TOP, TOK), F32),
            jax.ShapeDtypeStruct((slots, ffe), BF16),
            jax.ShapeDtypeStruct((ffe, model), BF16),
        ),
        in_specs=[vmem, vmem, vmem],
        out_specs=(hbm, hbm, hbm),
        scratch_shapes=[
            dma((13,)),
        ],
        compiler_params=pltpu.CompilerParams(vmem_limit_bytes=2 * 1024 * 1024),
        cost_estimate=pl.CostEstimate(
            flops=0, bytes_accessed=17_000_000, transcendentals=0
        ),
    )(grad_gates, grad_hidden, grad_down)
    return grad_gates.T, grad_hidden[None], grad_down[None]


def solution(mesh):
    both = ("dp", "tensor")
    in_specs = (P(both, None), P(both, None), P(both, None), P(both, None, None), P(both, None, None))
    out_specs = (P(both, None), P(both, None, None), P(both, None, None))
    return jax.shard_map(local, mesh=mesh, in_specs=in_specs, out_specs=out_specs, check_vma=False)
```
